128 devices in a mesh: rep: 8 (over z_lo, x), tp: 16 (over z_hi, y, core).
Axes of the slice: x: 4, y: 4, z: 4 (z_hi: 2, z_lo: 2; z = z_hi * 2 + z_lo), core: 2. Of those that a mesh axis runs over, the one named last changes fastest.
Arguments:
- step_token_index: int32 [4, 1024], replicated, may hold values from 0 to 75967
- row_tenant_index: int32 [1024], P('rep'), may hold values from 0 to 3
- stored_lengths: int32 [1024], P('rep'), may hold values from 1 to 192, as said below
- embedding: bfloat16 [75968, 5120], P('rep', 'tp'), may hold values from -6 to 6
- input_norm_gain: float32 [5120], replicated, may hold values from 0.1 to 1.9
- query_weight: bfloat16 [5120, 8192], P(None, 'tp'), may hold values from -0.078125 to 0.078125
- key_weight: bfloat16 [5120, 1024], P(None, 'tp'), may hold values from -0.078125 to 0.078125
- value_weight: bfloat16 [5120, 1024], P(None, 'tp'), may hold values from -0.078125 to 0.078125
- output_weight: bfloat16 [8192, 5120], P('tp'), may hold values from -0.0625 to 0.0625
- query_norm_gain: float32 [128], replicated, may hold values from 0.1 to 1.9
- key_norm_gain: float32 [128], replicated, may hold values from 0.1 to 1.9
- adapter_down_weight: bfloat16 [4, 5120, 128], P(None, 'tp', 'rep'), may hold values from -0.078125 to 0.078125
- adapter_up_weight: bfloat16 [4, 128, 8192], P(None, 'rep', 'tp'), may hold values from -0.5 to 0.5
- stored_keys: bfloat16 [1024, 1536, 128], P('rep', 'tp'), may hold values from -360 to 360
- stored_values: bfloat16 [1024, 1536, 128], P('rep', 'tp'), may hold values from -6 to 6
Outputs:
- layer_out: bfloat16 [4, 1024, 5120], P(None, 'rep', 'tp')
The draws below stay inside these ranges and needn't reach their ends.
Inputs may be any that keep to these rules, and one draw needn't show every extreme that they name: `stored_lengths`: some row of every draw has 192 cached positions and some row has 1.
All inputs are finite; a program needn't handle non-finite values.
Results may differ from the reference program's by a relative error of at most 0.015.
Values may be sent and summed in bfloat16 or wider, within the bound.
No kernel may reach another device: no remote copies, remote signals or barrier semaphores. Data moves between devices by JAX's collectives and lax.ppermute only.
A program may use at most 256 MiB of HBM per device.

```python
import math
import jax
import jax.numpy as jnp
import numpy as np
from jax import lax

MODEL_WIDTH = 5120
QUERY_HEADS = 64
KVH = 8
HEAD_WIDTH = 128
VOCAB = 75968
ADAPTER_RANK = 128
TENANT_COUNT = 4
STEPS = 4
LMAX = 192
ROWS_ALL = 1024


def draw_stored_lengths(key, part):
    key = jax.random.fold_in(key, 11)
    first_key, second_key = jax.random.split(key)
    base = jax.random.randint(first_key, (ROWS_ALL,), 1, LMAX + 1)
    chosen = jax.random.randint(second_key, (), 0, ROWS_ALL)
    index = jnp.arange(ROWS_ALL)
    base = jnp.where(index == chosen, LMAX, base)
    base = jnp.where(index == (chosen + 1) % ROWS_ALL, 1, base)
    return base.astype(jnp.int32)


def draw_stored_keys(key, part):
    key = jax.random.fold_in(key, 23)
    first_key = jax.random.fold_in(key, 0)
    entries = jnp.clip(jax.random.normal(first_key, (ROWS_ALL, KVH * LMAX, HEAD_WIDTH), jnp.float32), -6.0, 6.0)
    return entries.astype(jnp.bfloat16)


def plant(values, stream_key, smallest, top_value):
    longest = values.shape.index(max(values.shape))
    spots = []
    for shift in (0, 1):
        where = [jax.random.randint(jax.random.fold_in(stream_key, axis), (), 0, length) for axis, length in enumerate(values.shape)]
        where[longest] = (where[longest] + shift) % values.shape[longest]
        spots.append(tuple(where))
    return values.at[spots[0]].set(smallest).at[spots[1]].set(top_value)


def block_levels(key, shape, cuts, low, top_value):
    factor_of, own = 1.0, jax.random.fold_in(key, 6)
    for axis_at, blocks in cuts:
        steps = jnp.exp(jax.random.uniform(jax.random.fold_in(own, axis_at), (blocks,), jnp.float32, low / len(cuts), top_value / len(cuts)))
        factor_of = factor_of * jnp.repeat(steps, shape[axis_at] // blocks).reshape([-1 if axis == axis_at else 1 for axis in range(len(shape))])
    return factor_of


def wide_ids(own_key, extent, count, slope):
    portions = [min(1 << octave, count + 1 - (1 << octave)) * (1 << 20) // math.isqrt((1 << octave) ** slope) + 1 for octave in range((count + 1).bit_length()) if 1 << octave <= count]
    deviation = 1 + sum(portions) // (1 << 30)
    grid = np.cumsum(np.array([max(1, weight // deviation) for weight in portions]))
    ticket = jax.random.randint(jax.random.fold_in(own_key, 1), extent, 0, int(grid[len(portions) - 1]))
    start = jnp.left_shift(1, jnp.searchsorted(jnp.asarray(grid, jnp.int32), ticket, side="right").astype(jnp.int32))
    standing = start - 1 + jax.random.randint(jax.random.fold_in(own_key, 4), extent, 0, 1 << 30) % jnp.minimum(start, count + 1 - start)
    return jax.random.permutation(jax.random.fold_in(own_key, 2), count)[standing].astype(jnp.int32)


def noise(own_key, extent, scale, most, pieces=(), kind=jnp.bfloat16):
    level = block_levels(own_key, extent, pieces, -0.22, 0.18) if pieces else 1.0
    values = jax.random.normal(own_key, extent, jnp.float32) * scale * level
    return jnp.minimum(jnp.maximum(values, -most), most).astype(kind)


def setup_inputs(seed: int = 0) -> dict:
    keys = jax.random.split(jax.random.key(seed), 16)
    step_token_index = plant(wide_ids(keys[0], (STEPS, ROWS_ALL), VOCAB, 2), jax.random.fold_in(keys[0], 3), 0, VOCAB - 1).astype(jnp.int32)
    row_tenant_index = plant(jax.random.randint(keys[1], (ROWS_ALL,), 0, TENANT_COUNT), jax.random.fold_in(keys[1], 1), 0, TENANT_COUNT - 1).astype(jnp.int32)
    stored_lengths = draw_stored_lengths(jax.random.fold_in(keys[15], 71), 0)
    embedding = noise(keys[3], (VOCAB, MODEL_WIDTH), 1.0, 6.0, ((0, 8), (1, 16)))
    input_norm_gain = jnp.clip(1.0 + 0.18 * jax.random.normal(keys[4], (MODEL_WIDTH,), jnp.float32), 0.1, 1.9)
    query_weight = noise(keys[5], (MODEL_WIDTH, QUERY_HEADS * HEAD_WIDTH), MODEL_WIDTH ** -0.5, 0.078125, ((1, 16),))
    key_weight = noise(keys[6], (MODEL_WIDTH, KVH * HEAD_WIDTH), MODEL_WIDTH ** -0.5, 0.078125, ((1, 16),))
    value_weight = noise(keys[7], (MODEL_WIDTH, KVH * HEAD_WIDTH), MODEL_WIDTH ** -0.5, 0.078125, ((1, 16),))
    output_weight = noise(keys[8], (QUERY_HEADS * HEAD_WIDTH, MODEL_WIDTH), (QUERY_HEADS * HEAD_WIDTH) ** -0.5, 0.0625, ((0, 16),))
    query_norm_gain = jnp.clip(1.0 + 0.18 * jax.random.normal(keys[9], (HEAD_WIDTH,), jnp.float32), 0.1, 1.9)
    key_norm_gain = jnp.clip(1.0 + 0.18 * jax.random.normal(keys[10], (HEAD_WIDTH,), jnp.float32), 0.1, 1.9)
    adapter_down_weight = noise(keys[11], (TENANT_COUNT, MODEL_WIDTH, ADAPTER_RANK), MODEL_WIDTH ** -0.5, 0.078125, ((1, 16), (2, 8)))
    adapter_up_weight = noise(keys[12], (TENANT_COUNT, ADAPTER_RANK, QUERY_HEADS * HEAD_WIDTH), ADAPTER_RANK ** -0.5, 0.5, ((1, 8), (2, 16)))
    stored_keys = draw_stored_keys(jax.random.fold_in(keys[15], 71), 0)
    stored_values = noise(keys[14], (ROWS_ALL, KVH * LMAX, HEAD_WIDTH), 1.0, 6.0, ((0, 8), (1, 16)))
    return {"step_token_index": step_token_index, "row_tenant_index": row_tenant_index, "stored_lengths": stored_lengths, "embedding": embedding, "input_norm_gain": input_norm_gain, "query_weight": query_weight, "key_weight": key_weight, "value_weight": value_weight, "output_weight": output_weight, "query_norm_gain": query_norm_gain, "key_norm_gain": key_norm_gain, "adapter_down_weight": adapter_down_weight, "adapter_up_weight": adapter_up_weight, "stored_keys": stored_keys, "stored_values": stored_values}


epsilon = 1e-06
rope_base = 1000000.0
adapter_scale = 2.0
masked_score = -1e+30

def rms_scale(vector, gain):
    power = lax.optimization_barrier(jnp.mean(vector * vector, axis=-1, keepdims=True))
    return vector * lax.rsqrt(power + epsilon) * gain

def rotary(vector, position):
    half_dim = vector.shape[-1] // 2
    inverse = rope_base ** (-jnp.arange(half_dim, dtype=jnp.float32) / half_dim)
    angle = position.astype(jnp.float32)[..., None] * inverse
    cosine = jnp.cos(angle)
    sine = jnp.sin(angle)
    first = vector[..., :half_dim]
    second = vector[..., half_dim:]
    return jnp.concatenate([first * cosine - second * sine, second * cosine + first * sine], axis=-1)

def attend_block(query_heads, key_block, value_block, new_keys, new_values, lengths):
    step_count = query_heads.shape[0]
    score_scale = query_heads.shape[-1] ** (-0.5)
    query_wide = query_heads.astype(jnp.float32)
    cached = jnp.einsum('srhd,rpd->srhp', query_wide, key_block.astype(jnp.float32)) * score_scale
    position = jnp.arange(key_block.shape[1])
    valid = position[None, :] < lengths[:, None]
    cached = jnp.where(valid[None, :, None, :], cached, masked_score)
    fresh = jnp.einsum('srhd,trd->srht', query_wide, new_keys.astype(jnp.float32)) * score_scale
    order = jnp.arange(step_count)
    causal = order[None, :] <= order[:, None]
    fresh = jnp.where(causal[:, None, None, :], fresh, masked_score)
    peak = jnp.maximum(lax.optimization_barrier(jnp.max(cached, axis=-1)), lax.optimization_barrier(jnp.max(fresh, axis=-1)))
    cached_weight = jnp.exp(cached - peak[..., None])
    fresh_weight = jnp.exp(fresh - peak[..., None])
    total = lax.optimization_barrier(jnp.sum(cached_weight, axis=-1)) + lax.optimization_barrier(jnp.sum(fresh_weight, axis=-1))
    weighted = jnp.einsum('srhp,rpd->srhd', cached_weight, value_block.astype(jnp.float32))
    weighted = weighted + jnp.einsum('srht,trd->srhd', fresh_weight, new_values.astype(jnp.float32))
    return (weighted / total[..., None]).astype(jnp.bfloat16)

def reference(step_token_index, row_tenant_index, stored_lengths, embedding, input_norm_gain, query_weight, key_weight, value_weight, output_weight, query_norm_gain, key_norm_gain, adapter_down_weight, adapter_up_weight, stored_keys, stored_values):
    total_rows = STEPS * ROWS_ALL
    embedded = jnp.take(embedding, step_token_index, axis=0)
    embedded_wide = embedded.astype(jnp.float32)
    normalized_input = rms_scale(embedded_wide, input_norm_gain).astype(jnp.bfloat16).reshape(total_rows, MODEL_WIDTH)
    tenant_rows = jnp.tile(row_tenant_index, STEPS)
    tenant_picker = (tenant_rows[:, None] == jnp.arange(TENANT_COUNT)[None, :]).astype(jnp.float32)
    reduced_rank_rows = jnp.zeros((total_rows, ADAPTER_RANK), jnp.float32)
    for tenant_number in range(TENANT_COUNT):
        reduced_rank_rows = reduced_rank_rows + tenant_picker[:, tenant_number:tenant_number + 1] * jnp.dot(normalized_input, adapter_down_weight[tenant_number], preferred_element_type=jnp.float32)
    reduced_rank_rows = reduced_rank_rows.astype(jnp.bfloat16)
    adapter_delta = jnp.zeros((total_rows, QUERY_HEADS * HEAD_WIDTH), jnp.float32)
    for tenant_number in range(TENANT_COUNT):
        adapter_delta = adapter_delta + tenant_picker[:, tenant_number:tenant_number + 1] * jnp.dot(reduced_rank_rows, adapter_up_weight[tenant_number], preferred_element_type=jnp.float32)
    query_projected = jnp.dot(normalized_input, query_weight, preferred_element_type=jnp.float32) + adapter_scale * adapter_delta
    positions = (jnp.tile(stored_lengths, STEPS) + jnp.repeat(jnp.arange(STEPS), ROWS_ALL)).astype(jnp.int32)
    queries = rotary(rms_scale(query_projected.reshape(total_rows, QUERY_HEADS, HEAD_WIDTH), query_norm_gain), positions[:, None]).astype(jnp.bfloat16)
    key_proj = jnp.dot(normalized_input, key_weight, preferred_element_type=jnp.float32).astype(jnp.bfloat16)
    key_proj = lax.optimization_barrier(key_proj).astype(jnp.float32).reshape(total_rows, KVH, HEAD_WIDTH)
    value_new = jnp.dot(normalized_input, value_weight, preferred_element_type=jnp.float32).astype(jnp.bfloat16)
    key_new = rotary(rms_scale(key_proj, key_norm_gain), positions[:, None]).astype(jnp.bfloat16)
    per_group = QUERY_HEADS // KVH
    query_grouped = queries.reshape(STEPS, ROWS_ALL, KVH, per_group, HEAD_WIDTH).transpose(2, 0, 1, 3, 4)
    keys_grouped = stored_keys.reshape(ROWS_ALL, KVH, LMAX, HEAD_WIDTH).transpose(1, 0, 2, 3)
    values_grouped = stored_values.reshape(ROWS_ALL, KVH, LMAX, HEAD_WIDTH).transpose(1, 0, 2, 3)
    new_key_grouped = key_new.reshape(STEPS, ROWS_ALL, KVH, HEAD_WIDTH).transpose(2, 0, 1, 3)
    new_value_grouped = value_new.reshape(STEPS, ROWS_ALL, KVH, HEAD_WIDTH).transpose(2, 0, 1, 3)

    def one_group(packed):
        query_heads, key_block, value_block, new_keys, new_values = packed
        return attend_block(query_heads, key_block, value_block, new_keys, new_values, stored_lengths)
    attended = lax.map(one_group, (query_grouped, keys_grouped, values_grouped, new_key_grouped, new_value_grouped))
    attended = attended.transpose(1, 2, 0, 3, 4).reshape(total_rows, QUERY_HEADS * HEAD_WIDTH)
    projected = jnp.dot(attended, output_weight, preferred_element_type=jnp.float32)
    layer_out = embedded_wide.reshape(total_rows, MODEL_WIDTH) + projected
    return layer_out.astype(jnp.bfloat16).reshape(STEPS, ROWS_ALL, MODEL_WIDTH)
```

```python
import jax
import jax.numpy as jnp
from jax import lax
from jax.sharding import PartitionSpec as P

epsilon = 1e-06
rope_base = 1000000.0
adapter_scale = 2.0
masked_score = -1e30
slots = 128


def tp_route(dz, dy, dc):
    route = []
    for place in range(16):
        z, y, core = place // 8, place // 2 % 4, place % 2
        route.append((place, (z + dz) % 2 * 8 + (y + dy) % 4 * 2 + (core + dc) % 2))
    return route


def rep_route(dz, dx):
    return [(place, (place // 4 + dz) % 2 * 4 + (place + dx) % 4) for place in range(8)]


def to_tp(block, dz, dy):
    return lax.ppermute(block, "tp", tp_route(dz, dy, 0))


def to_partner(block):
    return lax.ppermute(block, "tp", tp_route(0, 0, 1))


def rope_tables(positions, half_dim):
    inverse = rope_base ** (-jnp.arange(half_dim, dtype=jnp.float32) / half_dim)
    angle = positions.astype(jnp.float32)[:, None] * inverse
    return jnp.cos(angle), jnp.sin(angle)


def rotate(first, second, cosine, sine):
    return first * cosine - second * sine, second * cosine + first * sine


def tn_dot(left, right):
    return lax.dot_general(left, right, (((0,), (0,)), ((), ())), preferred_element_type=jnp.float32)


def embed(tokens, table, me, replica_count):
    vocab_rows = table.shape[0]
    token_count = tokens.shape[1]
    owner = tokens // vocab_rows
    parts = jnp.arange(replica_count)
    counts = jnp.sum((owner[:, None, :] == parts[None, :, None]).astype(jnp.int32), axis=2)
    most = jnp.max(counts)
    own_tokens = lax.dynamic_slice_in_dim(tokens, me, 1, axis=0)
    wanted = jnp.concatenate([owner == me, own_tokens // vocab_rows == parts[:, None]], axis=0)
    earlier = jnp.arange(token_count)[:, None] < jnp.arange(token_count)[None, :]
    rank = jnp.dot(
        wanted.astype(jnp.bfloat16), earlier.astype(jnp.bfloat16), preferred_element_type=jnp.float32
    ).astype(jnp.int32)
    rank = jnp.where(wanted, rank, -1)
    local = tokens - me * vocab_rows

    def one_round(base):
        place = base + jnp.arange(slots)
        hit = rank[:replica_count, None, :] == place[None, :, None]
        listed = jnp.sum(jnp.where(hit, local[:, None, :] + 1, 0), axis=2) - 1
        chosen = (
            jnp.arange(vocab_rows)[:, None] == listed.reshape(1, replica_count * slots)
        ).astype(jnp.bfloat16)
        picked = tn_dot(table, chosen).astype(jnp.bfloat16)
        sent = picked.reshape(table.shape[1], replica_count, slots).transpose(1, 0, 2)
        got = lax.all_to_all(sent, "rep", 0, 0, tiled=True)
        spread = (rank[replica_count:, None, :] == place[None, :, None]).astype(jnp.bfloat16)
        flat = got.transpose(1, 0, 2).reshape(table.shape[1], replica_count * slots)
        return jnp.dot(
            flat,
            spread.reshape(replica_count * slots, token_count),
            preferred_element_type=jnp.float32,
        )

    def more(state):
        base, held = state
        return base + slots, held + one_round(base)

    _, held = lax.while_loop(lambda state: state[0] < most, more, (slots, one_round(0)))
    return held.astype(jnp.bfloat16)


def sum_over_chips(value):
    value = value + to_tp(value, 1, 0)
    return value + to_tp(value, 0, 1) + to_tp(value, 0, 2) + to_tp(value, 0, 3)


def gather_chips(own):
    rows = own.shape[0]
    half = rows // 2
    third = rows // 3 // 16 * 16
    left, right, across = to_tp(own, 0, 1), to_tp(own, 0, -1), to_tp(own, 1, 0)
    far_a = to_tp(left[:half], 0, 1)
    far_b = to_tp(right[half:], 0, -1)
    across_left_a = to_tp(across[:half], 0, 1)
    across_right_b = to_tp(across[half:], 0, -1)
    across_left_b = to_tp(left[half:], 1, 0)
    across_right_a = to_tp(right[:half], 1, 0)
    far = jnp.concatenate([far_a, far_b])
    across_left = jnp.concatenate([across_left_a, across_left_b])
    across_right = jnp.concatenate([across_right_a, across_right_b])
    across_far = jnp.concatenate(
        [
            to_tp(across_left[:third], 0, 1),
            to_tp(across_right[third : 2 * third], 0, -1),
            to_tp(far[2 * third :], 1, 0),
        ]
    )
    return {
        (0, 0): own,
        (0, 1): left,
        (0, 3): right,
        (1, 0): across,
        (0, 2): far,
        (1, 1): across_left,
        (1, 3): across_right,
        (1, 2): across_far,
    }


def scatter_chips(block):
    narrow = lambda value: value.astype(jnp.bfloat16)
    farthest = narrow(block(1, 2))
    rows = farthest.shape[0]
    half = rows // 2
    third = rows // 3 // 16 * 16
    got_left = to_tp(farthest[:third], 0, 1)
    got_right = to_tp(farthest[third : 2 * third], 0, -1)
    got_across = to_tp(farthest[2 * third :], 1, 0)

    def add(value, start, piece):
        size = piece.shape[0]
        middle = value[start : start + size] + piece.astype(jnp.float32)
        return jnp.concatenate([value[:start], middle, value[start + size :]])

    across_left = narrow(add(block(1, 1), 0, got_left))
    across_right = narrow(add(block(1, 3), third, got_right))
    far = narrow(add(block(0, 2), 2 * third, got_across))
    across_from_left = to_tp(across_left[:half], 0, 1)
    across_from_right = to_tp(across_right[half:], 0, -1)
    left_from_across = to_tp(across_left[half:], 1, 0)
    right_from_across = to_tp(across_right[:half], 1, 0)
    left_from_far = to_tp(far[:half], 0, 1)
    right_from_far = to_tp(far[half:], 0, -1)
    across = narrow(add(add(block(1, 0), 0, across_from_left), half, across_from_right))
    left = narrow(add(add(block(0, 1), half, left_from_across), 0, left_from_far))
    right = narrow(add(add(block(0, 3), 0, right_from_across), half, right_from_far))
    total = block(0, 0) + to_tp(left, 0, 1).astype(jnp.float32)
    total = total + to_tp(right, 0, -1).astype(jnp.float32)
    return total + to_tp(across, 1, 0).astype(jnp.float32)


def attend_part(queries, keys, values, first_position, lengths):
    score_scale = queries.shape[-1] ** (-0.5)
    scores = (
        jnp.einsum("rqd,rpd->rqp", queries, keys, preferred_element_type=jnp.float32) * score_scale
    )
    position = first_position + jnp.arange(keys.shape[1])
    scores = jnp.where((position[None, :] < lengths[:, None])[:, None, :], scores, masked_score)
    return scores, values


def on_device(
    step_token_index,
    row_tenant_index,
    stored_lengths,
    embedding,
    input_norm_gain,
    query_weight,
    key_weight,
    value_weight,
    output_weight,
    query_norm_gain,
    key_norm_gain,
    adapter_down_weight,
    adapter_up_weight,
    stored_keys,
    stored_values,
):
    replica_count = lax.axis_size("rep")
    step_count = step_token_index.shape[0]
    row_count = row_tenant_index.shape[0]
    half_rows = row_count // 2
    count = step_count * half_rows
    own_width = embedding.shape[1]
    chip_width = 2 * own_width
    width = input_norm_gain.shape[0]
    head_size = query_norm_gain.shape[0]
    half_dim = head_size // 2
    tenant_count, _, rank_part = adapter_down_weight.shape
    me = lax.axis_index("rep")
    tp = lax.axis_index("tp")
    core = tp % 2
    low = core == 0
    chip = tp // 2

    def ordered(own, other, axis=0):
        return jnp.where(
            low, jnp.concatenate([own, other], axis), jnp.concatenate([other, own], axis)
        )

    packed = jnp.concatenate(
        [adapter_down_weight.transpose(0, 2, 1), adapter_up_weight], axis=2
    ).reshape(tenant_count * rank_part, own_width + adapter_up_weight.shape[2])
    slices = [packed] + [
        lax.ppermute(packed, "rep", rep_route(far // 4, far % 4)) for far in range(1, replica_count)
    ]
    slices = jnp.concatenate(slices)
    other_slices = to_partner(slices)
    down_own, up_own = slices[:, :own_width], slices[:, own_width:]
    down_other, up_other = other_slices[:, :own_width], other_slices[:, own_width:]

    query_other = to_partner(query_weight)
    key_other, value_other = to_partner((key_weight.T, value_weight.T))
    output_other = to_partner(output_weight)
    mine = core * half_rows
    theirs = (1 - core) * half_rows
    keys_own = lax.dynamic_slice_in_dim(stored_keys, mine, half_rows, 0)
    values_own = lax.dynamic_slice_in_dim(stored_values, mine, half_rows, 0)
    keys_other = to_partner(lax.dynamic_slice_in_dim(stored_keys, theirs, half_rows, 0))
    values_other = to_partner(lax.dynamic_slice_in_dim(stored_values, theirs, half_rows, 0))
    lengths = lax.dynamic_slice_in_dim(stored_lengths, mine, half_rows, 0)
    tenants = jnp.tile(lax.dynamic_slice_in_dim(row_tenant_index, mine, half_rows, 0), step_count)

    tokens = step_token_index.reshape(step_count, replica_count, 2, half_rows)
    tokens = tokens.transpose(1, 2, 0, 3).reshape(replica_count, 2 * count)
    own_columns = embed(tokens, embedding, me, replica_count)
    kept = lax.dynamic_slice_in_dim(own_columns, core * count, count, 1)
    passed = lax.dynamic_slice_in_dim(own_columns, (1 - core) * count, count, 1)
    chip_block = ordered(kept, to_partner(passed))

    wide = chip_block.astype(jnp.float32)
    power = sum_over_chips(jnp.sum(wide * wide, axis=0, keepdims=True)) / width
    scale = lax.rsqrt(power + epsilon)

    def normed(block, place):
        gain = lax.dynamic_slice_in_dim(input_norm_gain, place * chip_width, chip_width, 0)
        return (block.astype(jnp.float32) * scale * gain[:, None]).astype(jnp.bfloat16)

    picker = tenants[None, :] == jnp.arange(tenant_count)[:, None]
    own_normed = normed(chip_block, chip)
    own_part = lax.dynamic_slice_in_dim(own_normed, core * own_width, own_width, 0)
    other_part = lax.dynamic_slice_in_dim(own_normed, (1 - core) * own_width, own_width, 0)
    reduced = jnp.dot(down_own, own_part, preferred_element_type=jnp.float32) + jnp.dot(
        down_other, other_part, preferred_element_type=jnp.float32
    )
    reduced = reduced.reshape(replica_count, tenant_count, rank_part, count)
    reduced = jnp.sum(jnp.where(picker[None, :, None, :], reduced, 0.0), axis=1)
    low_rank = sum_over_chips(reduced.reshape(replica_count * rank_part, count)).astype(
        jnp.bfloat16
    )
    low_rank = low_rank.reshape(replica_count, 1, rank_part, count)
    spread = jnp.where(picker[None, :, None, :], low_rank, jnp.bfloat16(0)).reshape(-1, count)

    blocks = gather_chips(chip_block)
    query_a = adapter_scale * tn_dot(spread, up_own)
    query_b = adapter_scale * tn_dot(spread, up_other)
    kv_weights = (key_weight.T, key_other, value_weight.T, value_other)
    kv = [jnp.zeros((count, half_dim), jnp.float32)] * 4
    z, y = chip // 4, chip % 4
    for (dz, dy), block in blocks.items():
        place = (z + dz) % 2 * 4 + (y - dy) % 4
        start = place * chip_width
        ready = normed(block, place)
        query_a = query_a + tn_dot(
            ready, lax.dynamic_slice_in_dim(query_weight, start, chip_width, 0)
        )
        query_b = query_b + tn_dot(
            ready, lax.dynamic_slice_in_dim(query_other, start, chip_width, 0)
        )
        for index, weight in enumerate(kv_weights):
            part = lax.dynamic_slice_in_dim(weight, start, chip_width, 1)
            kv[index] = kv[index] + lax.dot_general(
                ready, part, (((0,), (1,)), ((), ())), preferred_element_type=jnp.float32
            )

    positions = jnp.tile(lengths, step_count) + jnp.repeat(jnp.arange(step_count), half_rows)
    cosine, sine = rope_tables(positions, half_dim)
    query = jnp.concatenate([query_a, query_b], axis=1).reshape(count, -1, head_size)
    heads = query.shape[1]
    query_power = jnp.mean(query * query, axis=-1, keepdims=True)
    query = query * lax.rsqrt(query_power + epsilon) * query_norm_gain
    query = jnp.concatenate(
        rotate(query[..., :half_dim], query[..., half_dim:], cosine[:, None], sine[:, None]), axis=-1
    ).astype(jnp.bfloat16)
    kv = [part.astype(jnp.bfloat16) for part in kv]
    key_wide = lax.optimization_barrier(ordered(kv[0], kv[1], 1)).astype(jnp.float32)
    key_power = jnp.mean(key_wide * key_wide, axis=-1, keepdims=True)
    key_wide = key_wide * lax.rsqrt(key_power + epsilon) * key_norm_gain
    keys_new = jnp.concatenate(
        rotate(key_wide[:, :half_dim], key_wide[:, half_dim:], cosine, sine), axis=-1
    ).astype(jnp.bfloat16)
    values_new = ordered(kv[2], kv[3], 1)

    queries = query.reshape(step_count, half_rows, heads, head_size).transpose(1, 0, 2, 3)
    queries = queries.reshape(half_rows, step_count * heads, head_size)
    fresh_keys = keys_new.reshape(step_count, half_rows, head_size).transpose(1, 0, 2)
    fresh_values = values_new.reshape(step_count, half_rows, head_size).transpose(1, 0, 2)
    block_size = stored_keys.shape[1]
    score_scale = head_size ** (-0.5)

    def cached_scores(keys, first_position):
        scores = jnp.einsum("rqd,rpd->rqp", queries, keys, preferred_element_type=jnp.float32)
        valid = first_position + jnp.arange(block_size)[None, :] < lengths[:, None]
        return jnp.where(valid[:, None, :], scores * score_scale, masked_score)

    own_scores = cached_scores(keys_own, core * block_size)
    other_scores = cached_scores(keys_other, (1 - core) * block_size)
    fresh = jnp.einsum("rqd,rtd->rqt", queries, fresh_keys, preferred_element_type=jnp.float32)
    step_of = jnp.arange(step_count * heads) // heads
    causal = jnp.arange(step_count)[None, :] <= step_of[:, None]
    fresh = jnp.where(causal[None], fresh * score_scale, masked_score)
    peak = jnp.maximum(
        jnp.maximum(jnp.max(own_scores, axis=-1), jnp.max(other_scores, axis=-1)),
        jnp.max(fresh, axis=-1),
    )
    total = 0.0
    weighted = 0.0
    for scores, values in (
        (own_scores, values_own),
        (other_scores, values_other),
        (fresh, fresh_values),
    ):
        weight = jnp.exp(scores - peak[..., None])
        total = total + jnp.sum(weight, axis=-1)
        weighted = weighted + jnp.einsum(
            "rqp,rpd->rqd", weight, values, preferred_element_type=jnp.float32
        )
    attended = (weighted / total[..., None]).astype(jnp.bfloat16)
    attended = attended.reshape(half_rows, step_count, heads, head_size).transpose(1, 0, 2, 3)
    attended = attended.reshape(count, heads * head_size)
    attended_own, attended_other = jnp.split(attended, 2, axis=1)

    def out_block(dz, dy):
        start = ((z + dz) % 2 * 4 + (y + dy) % 4) * chip_width
        product = 0.0
        for weight, part in ((output_weight, attended_own), (output_other, attended_other)):
            columns = lax.dynamic_slice_in_dim(weight, start, chip_width, 1)
            product = product + lax.dot_general(
                columns, part, (((0,), (1,)), ((), ())), preferred_element_type=jnp.float32
            )
        return product

    projected = scatter_chips(out_block)
    summed = (chip_block.astype(jnp.float32) + projected).astype(jnp.bfloat16)
    summed = summed.reshape(2, own_width, count)
    kept = lax.dynamic_index_in_dim(summed, core, 0, keepdims=False)
    passed = lax.dynamic_index_in_dim(summed, 1 - core, 0, keepdims=False)
    both = jnp.where(
        low,
        jnp.stack([kept, to_partner(passed)]),
        jnp.stack([to_partner(passed), kept]),
    )
    result = both.reshape(2, own_width, step_count, half_rows).transpose(2, 0, 3, 1)
    return result.reshape(step_count, row_count, own_width)


def solution(mesh):
    return jax.shard_map(
        on_device,
        mesh=mesh,
        in_specs=(
            P(),
            P("rep"),
            P("rep"),
            P("rep", "tp"),
            P(),
            P(None, "tp"),
            P(None, "tp"),
            P(None, "tp"),
            P("tp", None),
            P(),
            P(),
            P(None, "tp", "rep"),
            P(None, "rep", "tp"),
            P("rep", "tp", None),
            P("rep", "tp", None),
        ),
        out_specs=P(None, "rep", "tp"),
        check_vma=False,
    )
```

```python
import jax
import jax.numpy as jnp
import numpy as np
from jax import lax
from jax.experimental import pallas as pl
from jax.experimental.pallas import tpu as pltpu
from jax.sharding import PartitionSpec as P

epsilon = 1e-06
rope_base = 1000000.0
adapter_scale = 2.0
masked_score = -1e30
slots = 128


def tp_route(dz, dy, dc):
    route = []
    for place in range(16):
        z, y, core = place // 8, place // 2 % 4, place % 2
        route.append((place, (z + dz) % 2 * 8 + (y + dy) % 4 * 2 + (core + dc) % 2))
    return route


def rep_route(dz, dx):
    return [(place, (place // 4 + dz) % 2 * 4 + (place + dx) % 4) for place in range(8)]


def to_tp(block, dz, dy):
    return lax.ppermute(block, "tp", tp_route(dz, dy, 0))


def to_partner(block):
    return lax.ppermute(block, "tp", tp_route(0, 0, 1))


def over_replicas(block):
    count = lax.axis_size("rep")
    copies = jnp.broadcast_to(block[None], (count, *block.shape))
    return lax.all_to_all(copies, "rep", 0, 0, tiled=True)


def rope_tables(positions, half_dim):
    inverse = rope_base ** (-jnp.arange(half_dim, dtype=jnp.float32) / half_dim)
    angle = positions.astype(jnp.float32)[:, None] * inverse
    return jnp.cos(angle), jnp.sin(angle)


f32 = jnp.float32
bf16 = jnp.bfloat16
i32 = jnp.int32
megabyte = 1 << 20


def shape_of(shape, dtype):
    return jax.ShapeDtypeStruct(shape, dtype)


def nn(left, right):
    return jnp.dot(left, right, preferred_element_type=f32)


def nt(left, right):
    return lax.dot_general(left, right, (((1,), (1,)), ((), ())), preferred_element_type=f32)


def whole(array):
    return pl.BlockSpec(array.shape, lambda *_: (0,) * len(array.shape))


def call(kernel, out_shape, operands, scalars=(), grid=(1,), in_specs=None, out_specs=None, **extra):
    if in_specs is None:
        in_specs = [None] * len(operands)
    in_specs = [spec or whole(operand) for spec, operand in zip(in_specs, operands)]
    if out_specs is None:
        out_specs = jax.tree.map(whole, out_shape)
    flops = extra.pop("flops", 1 << 20)
    scratch = extra.pop("scratch", [])
    room = extra.pop("room", 8)
    moved = sum(operand.size * operand.dtype.itemsize for operand in operands)
    return pl.pallas_call(
        kernel,
        out_shape=out_shape,
        grid_spec=pltpu.PrefetchScalarGridSpec(
            num_scalar_prefetch=len(scalars),
            grid=grid,
            in_specs=in_specs,
            out_specs=out_specs,
            scratch_shapes=scratch,
        ),
        compiler_params=pltpu.CompilerParams(vmem_limit_bytes=room * megabyte),
        cost_estimate=pl.CostEstimate(flops=flops, bytes_accessed=moved, transcendentals=0),
    )(*scalars, *operands)


def after(value, *others):
    def kernel(*refs):
        del refs

    anywhere = pl.BlockSpec(memory_space=pl.ANY)
    return pl.pallas_call(
        kernel,
        out_shape=shape_of(value.shape, value.dtype),
        in_specs=[anywhere] * (1 + len(others)),
        out_specs=anywhere,
        input_output_aliases={0: 0},
    )(value, *others)


def ranks(tokens, me, vocab_rows):
    parts, count = tokens.shape

    def kernel(me_ref, tokens_ref, rank_ref, most_ref):
        owner = tokens_ref[...] // vocab_rows
        own = tokens_ref[pl.ds(me_ref[0], 1), :] // vocab_rows
        from_part = lax.broadcasted_iota(i32, (parts, count), 0) == own
        wanted = jnp.concatenate([(owner == me_ref[0]).astype(f32), from_part.astype(f32)], axis=0)
        earlier = lax.broadcasted_iota(i32, (count, count), 0) < lax.broadcasted_iota(
            i32, (count, count), 1
        )
        rank = nn(wanted.astype(bf16), earlier.astype(f32).astype(bf16)).astype(i32)
        rank_ref[...] = jnp.where(wanted > 0, rank, -1)
        most = jnp.zeros((parts, 1), f32)
        for part in range(parts):
            found = jnp.sum((owner == part).astype(f32), axis=1, keepdims=True)
            most = jnp.maximum(most, found)
        most_ref[0] = jnp.max(most).astype(i32)

    return call(
        kernel,
        (shape_of((2 * parts, count), i32), shape_of((1,), i32)),
        (tokens,),
        scalars=(me.reshape(1),),
        out_specs=(
            whole(shape_of((2 * parts, count), i32)),
            pl.BlockSpec(memory_space=pltpu.SMEM),
        ),
    )


def pick(tokens, rank, table, me, base):
    parts, count = tokens.shape
    features, vocab_rows = table.shape
    tile, piece = 1280, 256
    steps = pl.cdiv(vocab_rows, tile)

    def kernel(me_ref, base_ref, tokens_ref, rank_ref, table_ref, out_ref, list_ref, total_ref):
        step = pl.program_id(0)

        @pl.when(step == 0)
        def _():
            place = base_ref[0] + lax.broadcasted_iota(i32, (slots, count), 0)
            for part in range(parts):
                local = tokens_ref[part : part + 1, :] - me_ref[0] * vocab_rows
                hit = (rank_ref[part : part + 1, :] == place).astype(f32).astype(bf16)
                inside = jnp.logical_and(local >= 0, local < vocab_rows)
                local = jnp.where(inside, local, 0)
                high = local // 128
                digits = jnp.concatenate(
                    [high, local - high * 128, jnp.ones((6, count), i32)], axis=0
                )
                found = nt(digits.astype(f32).astype(bf16), hit).astype(i32)
                name = found[0:1] * 128 + found[1:2]
                list_ref[part : part + 1, :] = jnp.where(found[2:3] > 0, name, -1)
            total_ref[...] = jnp.zeros_like(total_ref)

        def add(block):
            name = lax.broadcasted_iota(i32, (piece, slots), 0).astype(f32).astype(bf16)
            yes, no = jnp.ones((), bf16), jnp.zeros((), bf16)
            for part in range(0, parts, 2):
                chosen = []
                for side in (part, part + 1):
                    rows = []
                    for start in range(0, tile, piece):
                        wanted = list_ref[side : side + 1, :] - (step * tile + start)
                        wanted = jnp.clip(wanted, -1, piece).astype(f32).astype(bf16)
                        rows.append(jnp.where(name == wanted, yes, no))
                    chosen.append(jnp.concatenate(rows, axis=0))
                total_ref[:, part * slots : (part + 2) * slots] += nn(
                    block, jnp.concatenate(chosen, axis=1)
                )

        @pl.when(step < steps - 1)
        def _():
            add(table_ref[...])

        @pl.when(step == steps - 1)
        def _():
            lane = step * tile + lax.broadcasted_iota(i32, (1, tile), 1)
            add(jnp.where(lane < vocab_rows, table_ref[...].astype(f32), 0.0).astype(bf16))

        @pl.when(step == steps - 1)
        def _():
            for part in range(parts):
                out_ref[part] = total_ref[:, part * slots : (part + 1) * slots].astype(bf16)

    return call(
        kernel,
        shape_of((parts, features, slots), bf16),
        (tokens, rank, table),
        scalars=(me.reshape(1), base.reshape(1)),
        grid=(steps,),
        in_specs=[None, None, pl.BlockSpec((features, tile), lambda step, *_: (0, step))],
        scratch=[pltpu.VMEM((parts, slots), i32), pltpu.VMEM((features, parts * slots), f32)],
        flops=2 * features * vocab_rows * parts * slots,
        room=20,
    )


def place_slots(rank, got, base, others=()):
    parts, features, _ = got.shape
    count = rank.shape[1]

    def kernel(base_ref, rank_ref, got_ref, *refs):
        out_ref = refs[-1]
        place = base_ref[0] + lax.broadcasted_iota(i32, (slots, count), 0)
        total = jnp.zeros((features, count), f32)
        for part in range(parts):
            hit = rank_ref[parts + part : parts + part + 1, :] == place
            total += nn(got_ref[part], hit.astype(f32).astype(bf16))
        out_ref[0] = total[:, : count // 2].astype(bf16)
        out_ref[1] = total[:, count // 2 :].astype(bf16)

    return call(
        kernel,
        shape_of((2, features, count // 2), bf16),
        (rank, got, *others),
        scalars=(base.reshape(1),),
        in_specs=[None, None] + [pl.BlockSpec(memory_space=pl.ANY)] * len(others),
    )


def embed(tokens, table, me, before, beside):
    rank, most = ranks(tokens, me, table.shape[1])

    def more(state):
        base, held = state
        sent = pick(tokens, rank, table, me, base)
        got = lax.all_to_all(sent, "rep", 0, 0, tiled=True)
        return base + slots, held + place_slots(rank, got, base)

    base = jnp.zeros((), i32)
    sent = after(pick(tokens, rank, table, me, base), *before)
    got = lax.all_to_all(sent, "rep", 0, 0, tiled=True)
    beside = beside(before)
    first = place_slots(rank, got, base, beside)
    _, held = lax.while_loop(
        lambda state: state[0] < most[0], more, (jnp.full((), slots, i32), first)
    )
    return held, beside


def to_rows(core, kept, got):
    features, count = kept.shape

    def kernel(core_ref, kept_ref, got_ref, plain_ref, power_ref):
        low = core_ref[0] == 0
        kept, got = kept_ref[...].astype(f32), got_ref[...].astype(f32)
        both = jnp.concatenate([jnp.where(low, kept, got), jnp.where(low, got, kept)], axis=0)
        plain_ref[...] = both.T.astype(bf16)
        power = jnp.sum(both * both, axis=0, keepdims=True)
        for part in range(count // 128):
            power_ref[part : part + 1, :] = power[:, part * 128 : (part + 1) * 128]

    return call(
        kernel,
        (shape_of((count, 2 * features), bf16), shape_of((count // 128, 128), f32)),
        (kept, got),
        scalars=(core.reshape(1),),
    )


def across_chips(value):
    value = value + to_tp(value, 1, 0)
    for mask in (1, 3):
        route = [(place, place ^ (mask << 1)) for place in range(16)]
        value = value + lax.ppermute(value, "tp", route)
    return value


def reduce_own(core, chip, plain, power, gain, slices_own, slices_other, tenants):
    count, features = plain.shape
    width = gain.size
    parts, tenant_count, rank_part, packed_width = slices_own.shape
    skip = packed_width - features // 2

    def kernel(
        core_ref, chip_ref, plain_ref, power_ref, gain_ref, own_ref, other_ref, tenant_ref,
        scale_ref, out_ref,
    ):
        low = core_ref[0] == 0
        scale = lax.rsqrt(power_ref[...] / width + epsilon)
        scale = jnp.concatenate(
            [
                jnp.broadcast_to(scale[part : part + 1, :], (128, 128)).T
                for part in range(count // 128)
            ],
            axis=0,
        )
        scale_ref[...] = scale
        normed = (plain_ref[...].astype(f32) * scale[:, :1] * gain_ref[0]).astype(bf16)
        reduced = jnp.zeros((count, parts * rank_part), f32)
        for tenant in range(tenant_count):
            own = jnp.concatenate([own_ref[part, tenant, :, skip:] for part in range(parts)], axis=0)
            other = jnp.concatenate(
                [other_ref[part, tenant, :, skip:] for part in range(parts)], axis=0
            )
            own, other = own.astype(f32), other.astype(f32)
            down = jnp.concatenate(
                [jnp.where(low, own, other), jnp.where(low, other, own)], axis=1
            ).astype(bf16)
            reduced += jnp.where(tenant_ref[...] == tenant, nt(normed, down), 0.0)
        out_ref[...] = reduced

    return call(
        kernel,
        (shape_of((count, 128), f32), shape_of((count, parts * rank_part), f32)),
        (plain, power, gain, slices_own, slices_other, tenants),
        scalars=(core.reshape(1), chip.reshape(1)),
        in_specs=[
            None,
            None,
            pl.BlockSpec((1, 1, features), lambda step, core, chip: (chip[0], 0, 0)),
            None,
            None,
            None,
        ],
        flops=2 * features * count * parts * tenant_count * rank_part,
        room=12,
    )


def next_gather(left, right, across):
    half = left.shape[0] // 2

    def kernel(left_ref, right_ref, across_ref, up_ref, down_ref, over_ref):
        up_ref[:half] = left_ref[:half]
        up_ref[half:] = across_ref[:half]
        down_ref[:half] = right_ref[half:]
        down_ref[half:] = across_ref[half:]
        over_ref[:half] = left_ref[half:]
        over_ref[half:] = right_ref[:half]

    sent = shape_of(left.shape, bf16)
    return call(kernel, (sent, sent, sent), (left, right, across))


def last_gather(up, down, cut):
    count, features = up.shape
    half = count // 2
    first, second = cut

    def kernel(up_ref, down_ref, right_ref, left_ref, across_ref):
        right_ref[...] = up_ref[half : half + first]
        left_ref[...] = down_ref[second:]
        across_ref[: half - first] = up_ref[first:half]
        across_ref[half - first :] = down_ref[: second - half]

    return call(
        kernel,
        tuple(
            shape_of((rows, features), bf16) for rows in (first, count - second, second - first)
        ),
        (up, down),
    )


def project(places, pieces, scale, gain, weights, total=None, finish=None):
    arrays = []
    layout = []
    for piece in pieces:
        entry = []
        for array, start, rows in piece:
            known = [index for index, held in enumerate(arrays) if held is array]
            if not known:
                arrays.append(array)
                known = [len(arrays) - 1]
            entry.append((known[0], start, rows))
        layout.append(entry)
    count = sum(rows for _, _, rows in pieces[0])
    query_own, query_other, pairs = weights
    columns = query_own.shape[1]
    chip_width = query_own.shape[0] // 8
    has_total = total is not None
    steps = 2
    part = columns // steps
    many = len(pieces)

    def kernel(places_ref, *refs):
        del places_ref
        refs = list(refs)
        taken = [refs.pop(0) for _ in arrays]
        scale_ref = refs.pop(0)
        gain_refs = [refs.pop(0) for _ in pieces]
        own_refs = [refs.pop(0) for _ in pieces]
        other_refs = [refs.pop(0) for _ in pieces]
        pair_refs = [refs.pop(0) for _ in pieces]
        total_refs = [refs.pop(0) for _ in range(3)] if has_total else None
        finish_refs = [refs.pop(0) for _ in range(9)] if finish is not None else None
        outs, sums = (refs[:-3], refs[-3:]) if finish is not None else ([], refs)
        step = pl.program_id(0)
        rows = []
        for entry, gain_ref in zip(layout, gain_refs):
            plain = [taken[at][first : first + size] for at, first, size in entry]
            plain = jnp.concatenate(plain, axis=0).astype(f32)
            rows.append((plain * scale_ref[:, :1] * gain_ref[0]).astype(bf16))
        rows = jnp.concatenate(rows, axis=1)
        for side, weight_refs in enumerate((own_refs, other_refs)):
            result = nn(rows, jnp.concatenate([ref[...] for ref in weight_refs], axis=0))
            if has_total:
                result += total_refs[side][...]
            if finish is None:
                sums[side][...] = result
            else:
                sums[side][:, pl.ds(pl.multiple_of(step * part, part), part)] = result

        @pl.when(step == 0)
        def _():
            result = nt(rows, jnp.concatenate([ref[...] for ref in pair_refs], axis=1))
            if has_total:
                result += total_refs[2][...]
            sums[2][...] = result

        if finish is not None:

            @pl.when(step == steps - 1)
            def _():
                finish_kernel(finish_refs, sums, outs)

    def weight_spec(index):
        return pl.BlockSpec((chip_width, part), lambda step, places: (places[index], step))

    def pair_spec(index):
        return pl.BlockSpec((pairs.shape[0], chip_width), lambda step, places: (0, places[index]))

    sum_spec = pl.BlockSpec((count, part), lambda step, places: (0, step))
    sums = (
        shape_of((count, columns), f32),
        shape_of((count, columns), f32),
        shape_of((count, pairs.shape[0]), f32),
    )
    sum_specs = (sum_spec, sum_spec, whole(sums[2]))
    def gain_spec(index):
        return pl.BlockSpec((1, 1, chip_width), lambda step, places: (places[index], 0, 0))

    in_specs = [None] * (len(arrays) + 1)
    in_specs += [gain_spec(index) for index in range(many)]
    in_specs += [weight_spec(index) for index in range(many)] * 2
    in_specs += [pair_spec(index) for index in range(many)]
    operands = arrays + [scale] + [gain] * many + [query_own] * many + [query_other] * many + [pairs] * many
    if has_total:
        operands += list(total)
        in_specs += list(sum_specs)
    if finish is None:
        out_shape, out_specs, scratch = sums, sum_specs, []
    else:
        operands += list(finish)
        in_specs += [None] * 9
        out_shape = (
            shape_of((count, 2 * columns), f32),
            shape_of((count, pairs.shape[0] // 2), bf16),
            shape_of((count, pairs.shape[0] // 2), bf16),
        )
        out_specs = None
        scratch = [pltpu.VMEM(sum_.shape, f32) for sum_ in sums]
    return call(
        kernel,
        out_shape,
        operands,
        scalars=(places,),
        grid=(steps,),
        in_specs=in_specs,
        out_specs=out_specs,
        scratch=scratch,
        flops=2 * many * count * chip_width * (2 * columns + pairs.shape[0]),
        room=28,
    )


def finish_kernel(refs, sums, outs):
    core_ref, reduced_ref, tenant_ref, own_ref, other_ref, query_gain_ref, key_gain_ref = refs[:7]
    cosine, sine = refs[7][...], refs[8][...]
    out_query_ref, out_key_ref, out_value_ref = outs
    parts, tenant_count = own_ref.shape[:2]
    columns = sums[0].shape[1]
    low_rank = reduced_ref[...].astype(bf16).astype(f32)
    head_size = cosine.shape[1]

    def head_norm(vector, gain):
        power = jnp.mean(vector * vector, axis=-1, keepdims=True)
        vector = vector * lax.rsqrt(power + epsilon) * gain
        return vector * cosine + pltpu.roll(vector, head_size // 2, 1) * sine

    spread = jnp.concatenate(
        [
            jnp.where(tenant_ref[...] == tenant, low_rank, 0.0).astype(bf16)
            for tenant in range(tenant_count)
        ],
        axis=1,
    )
    for side, up_ref in enumerate((own_ref, other_ref)):
        up = jnp.concatenate(
            [
                up_ref[part, tenant, :, :columns]
                for tenant in range(tenant_count)
                for part in range(parts)
            ],
            axis=0,
        )
        delta = nn(spread, up)
        for head in range(columns // head_size):
            near = slice(head * head_size, (head + 1) * head_size)
            query = sums[side][:, near] + adapter_scale * delta[:, near]
            query = head_norm(query, query_gain_ref[...])
            spot = slice(side * columns + near.start, side * columns + near.stop)
            out_query_ref[:, spot] = query.astype(bf16).astype(f32)
    low = core_ref[0, 0] == 0
    both = sums[2][...]
    key = both[:, :head_size].astype(bf16).astype(f32)
    value = both[:, head_size:]
    key = jnp.where(low, key, pltpu.roll(key, head_size // 2, 1))
    value = jnp.where(low, value, pltpu.roll(value, head_size // 2, 1))
    out_key_ref[...] = head_norm(key, key_gain_ref[...]).astype(bf16)
    out_value_ref[...] = value.astype(bf16)


def allowed_below(block_size, step_count, group):
    table = np.full((2, 2, group * 2 * step_count, 4 * block_size + 4 * step_count), 1 << 20, np.int32)
    for row in range(table.shape[2]):
        pair_row, step = row // step_count % 2, row % step_count
        for core in range(2):
            for side in range(2):
                start = side * 2 * block_size + pair_row * block_size
                first = (core if side == 0 else 1 - core) * block_size
                table[core, :, row, start : start + block_size] = first + np.arange(block_size)
            for pair in range(2):
                start = 4 * block_size + (2 * pair + pair_row) * step_count
                table[core, pair, row, start : start + step + 1] = -1
    return table


def attend(core, lengths, query, new_keys, new_values, caches, step_count):
    count, query_width = query.shape
    block_size, head_size = caches[0].shape[1:]
    group = query_width // head_size
    rows_a_step = 8
    block = rows_a_step * step_count
    half_rows = count // step_count
    grid = half_rows // rows_a_step
    score_scale = head_size ** (-0.5)
    limits = allowed_below(block_size, step_count, group)

    def kernel(
        core_ref, lengths_ref, query_ref, new_key_ref, new_value_ref, own_key_ref, other_key_ref,
        own_value_ref, other_value_ref, limit_ref, out_ref,
    ):
        first = core_ref[0] * half_rows + pl.program_id(0) * rows_a_step
        pair_tokens = 2 * step_count
        pairs = range(rows_a_step // 2)
        row = lax.broadcasted_iota(i32, (group * pair_tokens, 1), 0) // step_count % 2
        fresh = [slice(pair // 2 * 4 * step_count, (pair // 2 + 1) * 4 * step_count) for pair in pairs]

        def joined(pair, own, other, new):
            near = 2 * pair
            return jnp.concatenate(
                [own[near], own[near + 1], other[near], other[near + 1], new[fresh[pair], :]], axis=0
            )

        scores = []
        for pair in pairs:
            tokens = slice(pair * pair_tokens, (pair + 1) * pair_tokens)
            queries = [
                query_ref[tokens, head * head_size : (head + 1) * head_size] for head in range(group)
            ]
            queries = jnp.concatenate(queries, axis=0).astype(bf16)
            scores.append(nt(queries, joined(pair, own_key_ref, other_key_ref, new_key_ref)))
        weights, totals = [], []
        for pair in pairs:
            length = jnp.where(
                row == 0, lengths_ref[first + 2 * pair], lengths_ref[first + 2 * pair + 1]
            )
            seen = limit_ref[0, pair % 2] < length
            masked = jnp.where(seen, scores[pair] * score_scale, masked_score)
            weight = jnp.exp(masked - jnp.max(masked, axis=1, keepdims=True))
            totals.append(jnp.sum(weight, axis=1, keepdims=True))
            weights.append(weight.astype(bf16))
        results = []
        for pair in pairs:
            values = joined(pair, own_value_ref, other_value_ref, new_value_ref)
            results.append(nn(weights[pair], values) / totals[pair])
        for pair in pairs[::2]:
            for head in range(group):
                part = slice(head * pair_tokens, (head + 1) * pair_tokens)
                both = jnp.concatenate([results[pair][part], results[pair + 1][part]], axis=0)
                out_ref[fresh[pair], head * head_size : (head + 1) * head_size] = both.astype(bf16)

    rows_spec = lambda width: pl.BlockSpec((block, width), lambda step, *_: (step, 0))
    cache_spec = pl.BlockSpec(
        (rows_a_step, block_size, head_size),
        lambda step, core_ref, lengths_ref: (core_ref[0] * grid + step, 0, 0),
    )
    limit_spec = pl.BlockSpec(
        (1, *limits.shape[1:]), lambda step, core_ref, lengths_ref: (core_ref[0], 0, 0, 0)
    )
    keys_own, keys_other, values_own, values_other = caches
    return call(
        kernel,
        shape_of((count, query_width), bf16),
        (query, new_keys, new_values, keys_own, keys_other, values_own, values_other, limits),
        scalars=(core.reshape(1), lengths),
        grid=(grid,),
        in_specs=[rows_spec(query_width), rows_spec(head_size), rows_spec(head_size)]
        + [cache_spec] * 4
        + [limit_spec],
        out_specs=rows_spec(query_width),
        room=16,
        flops=4 * count * query_width * 2 * 2 * block_size,
    )


def out_blocks(places, attended, own, other, cut=None):
    count, width = attended.shape
    steps = places.shape[0]
    depth = own.shape[0]
    chip_width = own.shape[1] // 8

    def kernel(places_ref, attended_ref, own_ref, other_ref, *out_refs):
        del places_ref
        weight = jnp.concatenate([own_ref[...], other_ref[...]], axis=0)
        product = nn(attended_ref[...], weight).astype(bf16)
        if cut is None:
            out_refs[0][0] = product
        else:
            for ref, start, stop in zip(out_refs, (0, *cut), (*cut, count)):
                ref[...] = product[start:stop]

    weight_spec = pl.BlockSpec((depth, chip_width), lambda step, places: (0, places[step]))
    if cut is None:
        out_shape = shape_of((steps, count, chip_width), bf16)
        out_specs = pl.BlockSpec((1, count, chip_width), lambda step, places: (step, 0, 0))
    else:
        sizes = (cut[0], cut[1] - cut[0], count - cut[1])
        out_shape = tuple(shape_of((size, chip_width), bf16) for size in sizes)
        out_specs = None
    return call(
        kernel,
        out_shape,
        (attended, own, other),
        scalars=(places,),
        grid=(steps,),
        in_specs=[None, weight_spec, weight_spec],
        out_specs=out_specs,
        flops=2 * steps * count * width * chip_width,
        room=16,
    )


def plus(value, piece):
    return (value.astype(f32) + piece.astype(f32)).astype(bf16)


def second_round(blocks, from_left, from_right, from_across, cut):
    _, count, features = blocks.shape
    half = count // 2
    first, second = cut

    def kernel(blocks_ref, left_ref, right_ref, across_ref, up_ref, down_ref, over_ref):
        far, across_left, across_right = blocks_ref.at[0], blocks_ref.at[1], blocks_ref.at[2]
        up_ref[:first] = plus(across_left[:first], left_ref[...])
        up_ref[first:half] = across_left[first:half]
        up_ref[half:] = far[:half]
        down_ref[: second - half] = plus(across_right[half:second], right_ref[half - first :])
        down_ref[second - half : half] = across_right[second:]
        down_ref[half : second] = far[half:second]
        down_ref[second:] = plus(far[second:], across_ref[...])
        over_ref[:half] = across_left[half:]
        over_ref[half : half + first] = across_right[:first]
        over_ref[half + first :] = plus(across_right[first:half], right_ref[: half - first])

    sent = shape_of((count, features), bf16)
    return call(kernel, (sent, sent, sent), (blocks, from_left, from_right, from_across))


def third_round(blocks, from_left, from_right, from_across):
    _, count, features = blocks.shape
    half = count // 2

    def kernel(blocks_ref, left_ref, right_ref, across_ref, up_ref, down_ref, over_ref):
        left, right, across = blocks_ref.at[0], blocks_ref.at[1], blocks_ref.at[2]
        over_ref[:half] = plus(across[:half], left_ref[:half])
        over_ref[half:] = plus(across[half:], right_ref[:half])
        up_ref[:half] = plus(left[:half], left_ref[half:])
        up_ref[half:] = plus(left[half:], across_ref[:half])
        down_ref[:half] = plus(right[:half], across_ref[half:])
        down_ref[half:] = plus(right[half:], right_ref[half:])

    sent = shape_of((count, features), bf16)
    return call(kernel, (sent, sent, sent), (blocks, from_left, from_right, from_across))


def add_residual(core, blocks, plain, arrived):
    count, features = plain.shape
    half = features // 2

    def kernel(core_ref, blocks_ref, plain_ref, up_ref, down_ref, over_ref, keep_ref, pass_ref):
        total = blocks_ref[0].astype(f32) + up_ref[...].astype(f32)
        total += down_ref[...].astype(f32) + over_ref[...].astype(f32)
        total = plain_ref[...].astype(f32) + total
        low = core_ref[0] == 0
        first, second = total[:, :half], total[:, half:]
        keep_ref[...] = jnp.where(low, first, second).astype(bf16)
        pass_ref[...] = jnp.where(low, second, first).astype(bf16)

    part = shape_of((count, half), bf16)
    own = pl.BlockSpec((1, count, features), lambda step, core_ref: (3, 0, 0))
    return call(
        kernel,
        (part, part),
        (blocks, plain, *arrived),
        scalars=(core.reshape(1),),
        in_specs=[own] + [None] * 4,
    )


def to_steps(core, kept, got, step_count):
    count, features = kept.shape
    half_rows = count // step_count
    row_count = 2 * half_rows

    def kernel(core_ref, kept_ref, got_ref, out_ref):
        low = core_ref[0] == 0
        kept, got = kept_ref[...].astype(f32), got_ref[...].astype(f32)
        both = jnp.concatenate([jnp.where(low, kept, got), jnp.where(low, got, kept)], axis=0)
        token = lax.broadcasted_iota(i32, (2 * count, 2 * count), 0)
        column = lax.broadcasted_iota(i32, (2 * count, 2 * count), 1)
        target = token % step_count * row_count + token // step_count
        order = (column == target).astype(f32).astype(bf16)
        turned = nn(both.T.astype(bf16), order)
        for step in range(step_count):
            out_ref[step] = turned[:, step * row_count : (step + 1) * row_count].astype(bf16)

    return call(
        kernel,
        shape_of((step_count, features, row_count), bf16),
        (kept, got),
        scalars=(core.reshape(1),),
    )


def on_device(
    step_token_index,
    row_tenant_index,
    stored_lengths,
    embedding,
    input_norm_gain,
    query_weight,
    key_weight,
    value_weight,
    output_weight,
    query_norm_gain,
    key_norm_gain,
    adapter_down_weight,
    adapter_up_weight,
    stored_keys,
    stored_values,
):
    replica_count = lax.axis_size("rep")
    step_count = step_token_index.shape[0]
    row_count = row_tenant_index.shape[0]
    half_rows = row_count // 2
    count = step_count * half_rows
    own_width = embedding.shape[1]
    chip_width = 2 * own_width
    head_size = query_norm_gain.shape[0]
    half_dim = head_size // 2
    tenant_count, _, rank_part = adapter_down_weight.shape
    me = lax.axis_index("rep")
    tp = lax.axis_index("tp")
    core = tp % 2
    chip = tp // 2

    packed = jnp.concatenate([adapter_up_weight, adapter_down_weight.transpose(0, 2, 1)], axis=2)
    key_own, value_own = key_weight.T, value_weight.T
    before = (
        over_replicas(packed),
        to_partner(query_weight),
        to_partner(key_own),
        to_partner(value_own),
    )

    def beside(before):
        slices, query_other, key_other, value_other = before
        mine = core * half_rows
        lengths = lax.dynamic_slice_in_dim(stored_lengths, mine, half_rows, 0)
        tenants = lax.dynamic_slice_in_dim(row_tenant_index, mine, half_rows, 0)
        tenants = jnp.repeat(tenants, step_count)[:, None]
        positions = (lengths[:, None] + jnp.arange(step_count)).reshape(count)
        cosine, sine = rope_tables(positions, half_dim)
        return (
            slices,
            to_partner(slices),
            query_other,
            jnp.concatenate([key_own, key_other, value_own, value_other]),
            to_partner(stored_keys),
            to_partner(stored_values),
            to_partner(output_weight),
            tenants,
            jnp.concatenate([cosine, cosine], axis=1),
            jnp.concatenate([-sine, sine], axis=1),
            input_norm_gain.reshape(8, 1, chip_width),
        )

    tokens = step_token_index.reshape(step_count, replica_count, 2, half_rows)
    tokens = tokens.transpose(1, 2, 3, 0).reshape(replica_count, 2 * count)
    held, beside = embed(tokens, embedding.T, me, before, beside)
    slices, slices_other, query_other, pairs, keys_other, values_other, output_other = beside[:7]
    tenants, cosine, sine, gain = beside[7:]
    kept = lax.dynamic_index_in_dim(held, core, 0, keepdims=False)
    passed = lax.dynamic_index_in_dim(held, 1 - core, 0, keepdims=False)
    own, power = to_rows(core, kept, to_partner(passed))

    z, y = chip // 4, chip % 4

    def places(*far):
        return jnp.stack([(z + dz) % 2 * 4 + (y + dy) % 4 for dz, dy in far])

    half = count // 2
    third = count // 3 // 16 * 16
    cut = (third, 2 * third)
    left, right, across = to_tp(own, 0, 1), to_tp(own, 0, -1), to_tp(own, 1, 0)
    power = across_chips(power)
    scale, reduced = reduce_own(core, chip, own, power, gain, slices, slices_other, tenants)
    reduced = across_chips(reduced)
    up, down, over = next_gather(left, right, across)
    up, down, over = to_tp(up, 0, 1), to_tp(down, 0, -1), to_tp(over, 1, 0)
    weights = (query_weight, query_other, pairs)
    total = project(
        places((0, 0), (0, -1), (0, 1), (1, 0)),
        [[(own, 0, count)], [(left, 0, count)], [(right, 0, count)], [(across, 0, count)]],
        scale,
        gain,
        weights,
    )
    last_up, last_down, last_over = last_gather(up, down, cut)
    last_up, last_down = to_tp(last_up, 0, 1), to_tp(last_down, 0, -1)
    last_over = to_tp(last_over, 1, 0)
    total = project(
        places((0, 2), (1, -1), (1, 1)),
        [
            [(up, 0, half), (down, 0, half)],
            [(up, half, half), (over, 0, half)],
            [(over, half, half), (down, half, half)],
        ],
        scale,
        gain,
        weights,
        total,
    )
    query, new_keys, new_values = project(
        places((1, 2)),
        [[(last_up, 0, third), (last_over, 0, third), (last_down, 0, count - 2 * third)]],
        scale,
        gain,
        weights,
        total,
        (
            core.reshape(1, 1),
            reduced,
            tenants,
            slices,
            slices_other,
            query_norm_gain[None],
            key_norm_gain[None],
            cosine,
            sine,
        ),
    )

    attended = attend(
        core,
        stored_lengths,
        query,
        new_keys,
        new_values,
        (stored_keys, keys_other, stored_values, values_other),
        step_count,
    )

    out_weights = attended, output_weight, output_other
    sent = out_blocks(places((1, 2)), *out_weights, cut)
    arrived = to_tp(sent[0], 0, 1), to_tp(sent[1], 0, -1), to_tp(sent[2], 1, 0)
    blocks = out_blocks(places((0, 2), (1, 1), (1, -1)), *out_weights)
    sent = second_round(blocks, *arrived, cut)
    arrived = to_tp(sent[0], 0, 1), to_tp(sent[1], 0, -1), to_tp(sent[2], 1, 0)
    blocks = out_blocks(places((0, 1), (0, -1), (1, 0), (0, 0)), *out_weights)
    sent = third_round(blocks, *arrived)
    arrived = to_tp(sent[0], 0, 1), to_tp(sent[1], 0, -1), to_tp(sent[2], 1, 0)
    kept, passed = add_residual(core, blocks, own, arrived)
    result = to_steps(core, kept, to_partner(passed), step_count)
    return result.transpose(0, 2, 1)


def solution(mesh):
    return jax.shard_map(
        on_device,
        mesh=mesh,
        in_specs=(
            P(),
            P("rep"),
            P("rep"),
            P("rep", "tp"),
            P(),
            P(None, "tp"),
            P(None, "tp"),
            P(None, "tp"),
            P("tp", None),
            P(),
            P(),
            P(None, "tp", "rep"),
            P(None, "rep", "tp"),
            P("rep", "tp", None),
            P("rep", "tp", None),
        ),
        out_specs=P(None, "rep", "tp"),
        check_vma=False,
    )
```

```python
import jax
import jax.numpy as jnp
import numpy as np
from jax import lax
from jax.experimental import pallas as pl
from jax.experimental.pallas import tpu as pltpu
from jax.sharding import PartitionSpec as P

epsilon = 1e-06
rope_base = 1000000.0
adapter_scale = 2.0
masked_score = -1e30
slots = 128


def tp_route(dz, dy, dc):
    route = []
    for place in range(16):
        z, y, core = place // 8, place // 2 % 4, place % 2
        route.append((place, (z + dz) % 2 * 8 + (y + dy) % 4 * 2 + (core + dc) % 2))
    return route


def rep_route(dz, dx):
    return [(place, (place // 4 + dz) % 2 * 4 + (place + dx) % 4) for place in range(8)]


def to_tp(block, dz, dy):
    return lax.ppermute(block, "tp", tp_route(dz, dy, 0))


def to_partner(block):
    return lax.ppermute(block, "tp", tp_route(0, 0, 1))


def over_replicas(block):
    count = lax.axis_size("rep")
    copies = jnp.broadcast_to(block[None], (count, *block.shape))
    return lax.all_to_all(copies, "rep", 0, 0, tiled=True)


f32 = jnp.float32
bf16 = jnp.bfloat16
i32 = jnp.int32
megabyte = 1 << 20


def shape_of(shape, dtype):
    return jax.ShapeDtypeStruct(shape, dtype)


def nn(left, right):
    return jnp.dot(left, right, preferred_element_type=f32)


def nt(left, right):
    return lax.dot_general(left, right, (((1,), (1,)), ((), ())), preferred_element_type=f32)


def whole(array):
    return pl.BlockSpec(array.shape, lambda *_: (0,) * len(array.shape))


def call(kernel, out_shape, operands, scalars=(), grid=(1,), in_specs=None, out_specs=None, **extra):
    if in_specs is None:
        in_specs = [None] * len(operands)
    in_specs = [spec or whole(operand) for spec, operand in zip(in_specs, operands)]
    if out_specs is None:
        out_specs = jax.tree.map(whole, out_shape)
    flops = extra.pop("flops", 1 << 20)
    scratch = extra.pop("scratch", [])
    room = extra.pop("room", 8)
    moved = sum(operand.size * operand.dtype.itemsize for operand in operands)
    return pl.pallas_call(
        kernel,
        out_shape=out_shape,
        grid_spec=pltpu.PrefetchScalarGridSpec(
            num_scalar_prefetch=len(scalars),
            grid=grid,
            in_specs=in_specs,
            out_specs=out_specs,
            scratch_shapes=scratch,
        ),
        compiler_params=pltpu.CompilerParams(vmem_limit_bytes=room * megabyte),
        cost_estimate=pl.CostEstimate(flops=flops, bytes_accessed=moved, transcendentals=0),
    )(*scalars, *operands)


def after(value, *others):
    def kernel(*refs):
        del refs

    anywhere = pl.BlockSpec(memory_space=pl.ANY)
    return pl.pallas_call(
        kernel,
        out_shape=shape_of(value.shape, value.dtype),
        in_specs=[anywhere] * (1 + len(others)),
        out_specs=anywhere,
        input_output_aliases={0: 0},
    )(value, *others)


def row_tables(core, lengths, tenants, step_count, head_size, *others):
    row_count = lengths.shape[0]
    count = row_count // 2 * step_count
    half_dim = head_size // 2
    inverse = rope_base ** (-np.arange(half_dim, dtype=np.float32) / np.float32(half_dim))
    inverse = np.concatenate([inverse, inverse]).astype(np.float32)[None]

    def kernel(core_ref, lengths_ref, tenants_ref, inverse_ref, *refs):
        out_ref = refs[-1]
        token = lax.broadcasted_iota(i32, (count, row_count), 0)
        row = lax.broadcasted_iota(i32, (count, row_count), 1)
        chosen = row == core_ref[0] * (row_count // 2) + token // step_count
        length = jnp.sum(jnp.where(chosen, lengths_ref[...], 0).astype(f32), axis=1, keepdims=True)
        tenant = jnp.sum(jnp.where(chosen, tenants_ref[...], 0).astype(f32), axis=1, keepdims=True)
        step = lax.broadcasted_iota(i32, (count, 1), 0) % step_count
        angle = (length + step.astype(f32)) * inverse_ref[...]
        lane = lax.broadcasted_iota(i32, (count, head_size), 1)
        out_ref[:, :head_size] = jnp.cos(angle)
        sine = jnp.sin(angle)
        out_ref[:, head_size : 2 * head_size] = jnp.where(lane < half_dim, -sine, sine)
        out_ref[:, 2 * head_size :] = jnp.broadcast_to(tenant, (count, head_size))

    return call(
        kernel,
        shape_of((count, 3 * head_size), f32),
        (lengths[None], tenants[None], inverse, *others),
        scalars=(core.reshape(1),),
        in_specs=[None] * 3 + [pl.BlockSpec(memory_space=pl.ANY)] * len(others),
    )


def ranks(tokens, me, vocab_rows):
    parts, count = tokens.shape

    def kernel(me_ref, tokens_ref, rank_ref, most_ref):
        owner = tokens_ref[...] // vocab_rows
        own = tokens_ref[pl.ds(me_ref[0], 1), :] // vocab_rows
        from_part = lax.broadcasted_iota(i32, (parts, count), 0) == own
        wanted = jnp.concatenate([(owner == me_ref[0]).astype(f32), from_part.astype(f32)], axis=0)
        earlier = lax.broadcasted_iota(i32, (count, count), 0) < lax.broadcasted_iota(
            i32, (count, count), 1
        )
        rank = nn(wanted.astype(bf16), earlier.astype(f32).astype(bf16)).astype(i32)
        rank_ref[...] = jnp.where(wanted > 0, rank, -1)
        most = jnp.zeros((parts, 1), f32)
        for part in range(parts):
            found = jnp.sum((owner == part).astype(f32), axis=1, keepdims=True)
            most = jnp.maximum(most, found)
        most_ref[0] = jnp.max(most).astype(i32)

    return call(
        kernel,
        (shape_of((2 * parts, count), i32), shape_of((1,), i32)),
        (tokens,),
        scalars=(me.reshape(1),),
        out_specs=(
            whole(shape_of((2 * parts, count), i32)),
            pl.BlockSpec(memory_space=pltpu.SMEM),
        ),
    )


def pick(tokens, rank, table, me, base):
    parts, count = tokens.shape
    features, vocab_rows = table.shape
    tile, piece = 1280, 256
    steps = pl.cdiv(vocab_rows, tile)

    def kernel(me_ref, base_ref, tokens_ref, rank_ref, table_ref, out_ref, list_ref, total_ref):
        step = pl.program_id(0)

        @pl.when(step == 0)
        def _():
            place = base_ref[0] + lax.broadcasted_iota(i32, (slots, count), 0)
            for part in range(parts):
                local = tokens_ref[part : part + 1, :] - me_ref[0] * vocab_rows
                hit = (rank_ref[part : part + 1, :] == place).astype(f32).astype(bf16)
                inside = jnp.logical_and(local >= 0, local < vocab_rows)
                local = jnp.where(inside, local, 0)
                high = local // 128
                digits = jnp.concatenate(
                    [high, local - high * 128, jnp.ones((6, count), i32)], axis=0
                )
                found = nt(digits.astype(f32).astype(bf16), hit).astype(i32)
                name = found[0:1] * 128 + found[1:2]
                list_ref[part : part + 1, :] = jnp.where(found[2:3] > 0, name, -1)
            total_ref[...] = jnp.zeros_like(total_ref)

        def add(block):
            name = lax.broadcasted_iota(i32, (piece, slots), 0).astype(f32).astype(bf16)
            yes, no = jnp.ones((), bf16), jnp.zeros((), bf16)
            for part in range(0, parts, 2):
                chosen = []
                for side in (part, part + 1):
                    rows = []
                    for start in range(0, tile, piece):
                        wanted = list_ref[side : side + 1, :] - (step * tile + start)
                        wanted = jnp.clip(wanted, -1, piece).astype(f32).astype(bf16)
                        rows.append(jnp.where(name == wanted, yes, no))
                    chosen.append(jnp.concatenate(rows, axis=0))
                total_ref[:, part * slots : (part + 2) * slots] += nn(
                    block, jnp.concatenate(chosen, axis=1)
                )

        @pl.when(step < steps - 1)
        def _():
            add(table_ref[...])

        @pl.when(step == steps - 1)
        def _():
            lane = step * tile + lax.broadcasted_iota(i32, (1, tile), 1)
            add(jnp.where(lane < vocab_rows, table_ref[...].astype(f32), 0.0).astype(bf16))

        @pl.when(step == steps - 1)
        def _():
            for part in range(parts):
                out_ref[part] = total_ref[:, part * slots : (part + 1) * slots].astype(bf16)

    return call(
        kernel,
        shape_of((parts, features, slots), bf16),
        (tokens, rank, table),
        scalars=(me.reshape(1), base.reshape(1)),
        grid=(steps,),
        in_specs=[None, None, pl.BlockSpec((features, tile), lambda step, *_: (0, step))],
        scratch=[pltpu.VMEM((parts, slots), i32), pltpu.VMEM((features, parts * slots), f32)],
        flops=2 * features * vocab_rows * parts * slots,
        room=12,
    )


def place_slots(core, rank, got, base, others=()):
    parts, features, _ = got.shape
    count = rank.shape[1]
    half = count // 2

    def kernel(core_ref, base_ref, rank_ref, got_ref, *refs):
        kept_ref, passed_ref = refs[-2:]
        place = base_ref[0] + lax.broadcasted_iota(i32, (slots, count), 0)
        total = jnp.zeros((features, count), f32)
        for part in range(parts):
            hit = rank_ref[parts + part : parts + part + 1, :] == place
            total += nn(got_ref[part], hit.astype(f32).astype(bf16))
        low = core_ref[0] == 0
        first, second = total[:, :half], total[:, half:]
        kept_ref[...] = jnp.where(low, first, second).astype(bf16)
        passed_ref[...] = jnp.where(low, second, first).astype(bf16)

    columns = shape_of((features, half), bf16)
    return call(
        kernel,
        (columns, columns),
        (rank, got, *others),
        scalars=(core.reshape(1), base.reshape(1)),
        in_specs=[None, None] + [pl.BlockSpec(memory_space=pl.ANY)] * len(others),
    )


def embed(tokens, table, me, core, before, beside):
    rank, most = ranks(tokens, me, table.shape[1])

    def more(state):
        base, kept, passed = state
        sent = pick(tokens, rank, table, me, base)
        got = lax.all_to_all(sent, "rep", 0, 0, tiled=True)
        more_kept, more_passed = place_slots(core, rank, got, base)
        return base + slots, kept + more_kept, passed + more_passed

    base = jnp.zeros((), i32)
    picked = pick(tokens, rank, table, me, base)
    sent = after(picked, before)
    got = lax.all_to_all(sent, "rep", 0, 0, tiled=True)
    beside = beside(sent)
    first = place_slots(core, rank, got, base, beside)
    _, kept, passed = lax.while_loop(
        lambda state: state[0] < most[0], more, (jnp.full((), slots, i32), *first)
    )
    return kept, passed, beside


def to_rows(core, kept, got):
    features, count = kept.shape

    def kernel(core_ref, kept_ref, got_ref, plain_ref, power_ref):
        low = core_ref[0] == 0
        kept, got = kept_ref[...].astype(f32), got_ref[...].astype(f32)
        both = jnp.concatenate([jnp.where(low, kept, got), jnp.where(low, got, kept)], axis=0)
        plain_ref[...] = both.T.astype(bf16)
        power = jnp.sum(both * both, axis=0, keepdims=True)
        for part in range(count // 128):
            power_ref[part : part + 1, :] = power[:, part * 128 : (part + 1) * 128]

    return call(
        kernel,
        (shape_of((count, 2 * features), bf16), shape_of((count // 128, 128), f32)),
        (kept, got),
        scalars=(core.reshape(1),),
    )


def stack_pairs(key, value, other, ready):
    rows, columns = key.shape
    tile = columns // 4

    def kernel(key_ref, value_ref, other_ref, ready_ref, out_ref):
        del ready_ref
        out_ref[:rows] = key_ref[...]
        out_ref[rows : 2 * rows] = other_ref[:rows]
        out_ref[2 * rows : 3 * rows] = value_ref[...]
        out_ref[3 * rows :] = other_ref[rows:]

    tall = lambda many: pl.BlockSpec((many * rows, tile), lambda step: (0, step))
    return call(
        kernel,
        shape_of((4 * rows, columns), bf16),
        (key, value, other, ready),
        grid=(4,),
        in_specs=[tall(1), tall(1), tall(2), pl.BlockSpec(memory_space=pl.ANY)],
        out_specs=tall(4),
    )


def to_other_side(value, mask):
    route = [(place, place ^ (mask << 1)) for place in range(16)]
    return lax.ppermute(value, "tp", route)


def reduce_own(core, chip, plain, power, gain, slices, tables, *others):
    count, features = plain.shape
    width = gain.size
    parts, tenant_count, rank_part, packed_width = slices[0].shape
    skip = packed_width - features // 2

    def kernel(
        core_ref, chip_ref, plain_ref, power_ref, gain_ref, own_ref, other_ref, tables_ref, *refs,
    ):
        scale_ref, out_ref = refs[-2:]
        tenant_rows = tables_ref[:, 2 * 128 :]
        low = core_ref[0] == 0
        scale = lax.rsqrt(power_ref[...] / width + epsilon)
        scale = jnp.concatenate(
            [
                jnp.broadcast_to(scale[part : part + 1, :], (128, 128)).T
                for part in range(count // 128)
            ],
            axis=0,
        )
        scale_ref[...] = scale
        normed = (plain_ref[...].astype(f32) * scale[:, :1] * gain_ref[0]).astype(bf16)
        reduced = jnp.zeros((count, parts * rank_part), f32)
        for tenant in range(tenant_count):
            own, other = [
                jnp.concatenate([ref[part, tenant, :, skip:] for part in range(parts)], axis=0)
                for ref in (own_ref, other_ref)
            ]
            own, other = own.astype(f32), other.astype(f32)
            down = jnp.concatenate(
                [jnp.where(low, own, other), jnp.where(low, other, own)], axis=1
            ).astype(bf16)
            reduced += jnp.where(tenant_rows == tenant, nt(normed, down), 0.0)
        out_ref[...] = reduced

    return call(
        kernel,
        (shape_of((count, 128), f32), shape_of((count, parts * rank_part), f32)),
        (plain, power, gain, *slices, tables, *others),
        scalars=(core.reshape(1), chip.reshape(1)),
        in_specs=[
            None,
            None,
            pl.BlockSpec((1, 1, features), lambda step, core, chip: (chip[0], 0, 0)),
        ]
        + [None] * 3
        + [pl.BlockSpec(memory_space=pl.ANY)] * len(others),
        flops=2 * features * count * parts * tenant_count * rank_part,
        room=12,
    )


def next_gather(own, left, right, across, *others):
    count, features = left.shape
    half = count // 2

    def kernel(own_ref, left_ref, right_ref, across_ref, *refs):
        up_ref, down_ref, over_ref, near_ref = refs[-4:]
        up_ref[:half] = left_ref[:half]
        up_ref[half:] = across_ref[:half]
        down_ref[:half] = right_ref[half:]
        down_ref[half:] = across_ref[half:]
        over_ref[:half] = left_ref[half:]
        over_ref[half:] = right_ref[:half]
        for index, ref in enumerate((own_ref, left_ref, right_ref, across_ref)):
            near_ref[:, index * features : (index + 1) * features] = ref[...]

    sent = shape_of(left.shape, bf16)
    return call(
        kernel,
        (sent, sent, sent, shape_of((count, 4 * features), bf16)),
        (own, left, right, across, *others),
        in_specs=[None] * 4 + [pl.BlockSpec(memory_space=pl.ANY)] * len(others),
    )


def last_gather(up, down, cut):
    count, features = up.shape
    half = count // 2
    first, second = cut

    def kernel(up_ref, down_ref, right_ref, left_ref, across_ref):
        right_ref[...] = up_ref[half : half + first]
        left_ref[...] = down_ref[second:]
        across_ref[: half - first] = up_ref[first:half]
        across_ref[half - first :] = down_ref[: second - half]

    return call(
        kernel,
        tuple(
            shape_of((rows, features), bf16) for rows in (first, count - second, second - first)
        ),
        (up, down),
    )


def project(places, pieces, scale, gain, weights, total=None, others=()):
    arrays = []
    layout = []
    for piece in pieces:
        entry = []
        for array, start, rows in piece:
            known = [index for index, held in enumerate(arrays) if held is array]
            if not known:
                arrays.append(array)
                known = [len(arrays) - 1]
            entry.append((known[0], start, rows))
        layout.append(entry)
    count = scale.shape[0]
    query_own, query_other, pairs = weights
    columns = query_own.shape[1]
    chip_width = query_own.shape[0] // 8
    has_total = total is not None
    steps = 2
    part = columns // steps
    many = len(pieces)

    def kernel(places_ref, *refs):
        del places_ref
        refs = list(refs)
        taken = [refs.pop(0) for _ in arrays]
        scale_ref = refs.pop(0)
        gain_refs = [refs.pop(0) for _ in pieces]
        own_refs = [refs.pop(0) for _ in pieces]
        other_refs = [refs.pop(0) for _ in pieces]
        pair_refs = [refs.pop(0) for _ in pieces]
        total_refs = [refs.pop(0) for _ in range(3)] if has_total else None
        sums = refs[-3:]
        step = pl.program_id(0)
        rows = []
        for entry, gain_ref in zip(layout, gain_refs):
            plain = [
                taken[at][:, first : first + chip_width]
                if size is None
                else taken[at][first : first + size]
                for at, first, size in entry
            ]
            plain = jnp.concatenate(plain, axis=0).astype(f32)
            rows.append((plain * scale_ref[:, :1] * gain_ref[0]).astype(bf16))
        rows = jnp.concatenate(rows, axis=1)
        for side, weight_refs in enumerate((own_refs, other_refs)):
            result = nn(rows, jnp.concatenate([ref[...] for ref in weight_refs], axis=0))
            if has_total:
                result += total_refs[side][...]
            sums[side][...] = result

        @pl.when(step == 0)
        def _():
            result = nt(rows, jnp.concatenate([ref[...] for ref in pair_refs], axis=1))
            if has_total:
                result += total_refs[2][...]
            sums[2][...] = result

    def weight_spec(index):
        return pl.BlockSpec((chip_width, part), lambda step, places: (places[index], step))

    def pair_spec(index):
        return pl.BlockSpec((pairs.shape[0], chip_width), lambda step, places: (0, places[index]))

    sum_spec = pl.BlockSpec((count, part), lambda step, places: (0, step))
    sums = (
        shape_of((count, columns), f32),
        shape_of((count, columns), f32),
        shape_of((count, pairs.shape[0]), f32),
    )
    sum_specs = (sum_spec, sum_spec, whole(sums[2]))
    def gain_spec(index):
        return pl.BlockSpec((1, 1, chip_width), lambda step, places: (places[index], 0, 0))

    in_specs = [None] * (len(arrays) + 1)
    in_specs += [gain_spec(index) for index in range(many)]
    in_specs += [weight_spec(index) for index in range(many)] * 2
    in_specs += [pair_spec(index) for index in range(many)]
    operands = arrays + [scale] + [gain] * many + [query_own] * many + [query_other] * many + [pairs] * many
    if has_total:
        operands += list(total)
        in_specs += list(sum_specs)
    operands += list(others)
    in_specs += [pl.BlockSpec(memory_space=pl.ANY)] * len(others)
    return call(
        kernel,
        sums,
        operands,
        scalars=(places,),
        grid=(steps,),
        in_specs=in_specs,
        out_specs=sum_specs,
        flops=2 * many * count * chip_width * (2 * columns + pairs.shape[0]),
        room=18,
    )


def add(value, piece, *others):
    def kernel(value_ref, piece_ref, *refs):
        refs[-1][...] = value_ref[...] + piece_ref[...]

    return call(
        kernel,
        shape_of(value.shape, value.dtype),
        (value, piece, *others),
        in_specs=[None, None] + [pl.BlockSpec(memory_space=pl.ANY)] * len(others),
    )


def finish(core, query_own, query_other, kv, reduced, got, slices, query_gain, key_gain, tables):
    count, columns = query_own.shape

    def kernel(core_ref, own_ref, other_ref, kv_ref, *refs):
        finish_kernel(core_ref, (own_ref, other_ref), kv_ref, refs[:7], refs[7:])

    rows = shape_of((count, kv.shape[1] // 2), bf16)
    return call(
        kernel,
        (shape_of((count, 2 * columns), f32), rows, rows),
        (query_own, query_other, kv, reduced, got, *slices, query_gain, key_gain, tables),
        scalars=(core.reshape(1),),
        flops=2 << 30,
        room=16,
    )


def finish_kernel(core_ref, query_refs, kv_ref, refs, outs):
    reduced_ref, got_ref, *slice_refs = refs[:4]
    query_gain_ref, key_gain_ref, tables_ref = refs[4:]
    head_size = query_gain_ref.shape[1]
    cosine, sine = tables_ref[:, :head_size], tables_ref[:, head_size : 2 * head_size]
    tenant_rows = tables_ref[:, 2 * head_size :]
    out_query_ref, out_key_ref, out_value_ref = outs
    parts, tenant_count = slice_refs[0].shape[:2]
    columns = query_refs[0].shape[1]
    low_rank = (reduced_ref[...] + got_ref[...]).astype(bf16).astype(f32)
    def head_norm(vector, gain):
        power = jnp.mean(vector * vector, axis=-1, keepdims=True)
        vector = vector * lax.rsqrt(power + epsilon) * gain
        return vector * cosine + pltpu.roll(vector, head_size // 2, 1) * sine

    spread = jnp.concatenate(
        [
            jnp.where(tenant_rows == tenant, low_rank, 0.0).astype(bf16)
            for tenant in range(tenant_count)
        ],
        axis=1,
    )
    for side, up_ref in enumerate(slice_refs):
        up = jnp.concatenate(
            [
                up_ref[part, tenant, :, :columns]
                for tenant in range(tenant_count)
                for part in range(parts)
            ],
            axis=0,
        )
        delta = nn(spread, up)
        for head in range(columns // head_size):
            near = slice(head * head_size, (head + 1) * head_size)
            spot = slice(side * columns + near.start, side * columns + near.stop)
            query = query_refs[side][:, near] + adapter_scale * delta[:, near]
            query = head_norm(query, query_gain_ref[...])
            out_query_ref[:, spot] = query.astype(bf16).astype(f32)
    low = core_ref[0] == 0
    both = kv_ref[...]
    key = both[:, :head_size].astype(bf16).astype(f32)
    value = both[:, head_size:]
    key = jnp.where(low, key, pltpu.roll(key, head_size // 2, 1))
    value = jnp.where(low, value, pltpu.roll(value, head_size // 2, 1))
    out_key_ref[...] = head_norm(key, key_gain_ref[...]).astype(bf16)
    out_value_ref[...] = value.astype(bf16)


def allowed_below(block_size, step_count, group):
    table = np.full((2, 2, group * 2 * step_count, 4 * block_size + 4 * step_count), 1 << 20, np.int32)
    for row in range(table.shape[2]):
        pair_row, step = row // step_count % 2, row % step_count
        for core in range(2):
            for side in range(2):
                start = side * 2 * block_size + pair_row * block_size
                first = (core if side == 0 else 1 - core) * block_size
                table[core, :, row, start : start + block_size] = first + np.arange(block_size)
            for pair in range(2):
                start = 4 * block_size + (2 * pair + pair_row) * step_count
                table[core, pair, row, start : start + step + 1] = -1
    return table


def attend(core, lengths, query, new_keys, new_values, caches, step_count):
    count, query_width = query.shape
    block_size, head_size = caches[0].shape[1:]
    group = query_width // head_size
    rows_a_step = 8
    block = rows_a_step * step_count
    half_rows = count // step_count
    grid = half_rows // rows_a_step
    score_scale = head_size ** (-0.5)
    limits = allowed_below(block_size, step_count, group)

    def kernel(
        core_ref, lengths_ref, query_ref, new_key_ref, new_value_ref, own_key_ref, other_key_ref,
        own_value_ref, other_value_ref, limit_ref, out_ref,
    ):
        first = core_ref[0] * half_rows + pl.program_id(0) * rows_a_step
        pair_tokens = 2 * step_count
        pairs = range(rows_a_step // 2)
        row = lax.broadcasted_iota(i32, (group * pair_tokens, 1), 0) // step_count % 2
        fresh = [slice(pair // 2 * 4 * step_count, (pair // 2 + 1) * 4 * step_count) for pair in pairs]

        def joined(pair, own, other, new):
            near = 2 * pair
            return jnp.concatenate(
                [own[near], own[near + 1], other[near], other[near + 1], new[fresh[pair], :]], axis=0
            )

        scores = []
        for pair in pairs:
            tokens = slice(pair * pair_tokens, (pair + 1) * pair_tokens)
            queries = [
                query_ref[tokens, head * head_size : (head + 1) * head_size] for head in range(group)
            ]
            queries = jnp.concatenate(queries, axis=0).astype(bf16)
            scores.append(nt(queries, joined(pair, own_key_ref, other_key_ref, new_key_ref)))
        weights, totals = [], []
        for pair in pairs:
            length = jnp.where(
                row == 0, lengths_ref[first + 2 * pair], lengths_ref[first + 2 * pair + 1]
            )
            seen = limit_ref[0, pair % 2] < length
            masked = jnp.where(seen, scores[pair] * score_scale, masked_score)
            weight = jnp.exp(masked - jnp.max(masked, axis=1, keepdims=True))
            totals.append(jnp.sum(weight, axis=1, keepdims=True))
            weights.append(weight.astype(bf16))
        results = []
        for pair in pairs:
            values = joined(pair, own_value_ref, other_value_ref, new_value_ref)
            results.append(nn(weights[pair], values) / totals[pair])
        for pair in pairs[::2]:
            for head in range(group):
                part = slice(head * pair_tokens, (head + 1) * pair_tokens)
                both = jnp.concatenate([results[pair][part], results[pair + 1][part]], axis=0)
                out_ref[fresh[pair], head * head_size : (head + 1) * head_size] = both.astype(bf16)

    rows_spec = lambda width: pl.BlockSpec((block, width), lambda step, *_: (step, 0))
    cache_spec = pl.BlockSpec(
        (rows_a_step, block_size, head_size),
        lambda step, core_ref, lengths_ref: (core_ref[0] * grid + step, 0, 0),
    )
    limit_spec = pl.BlockSpec(
        (1, *limits.shape[1:]), lambda step, core_ref, lengths_ref: (core_ref[0], 0, 0, 0)
    )
    keys_own, keys_other, values_own, values_other = caches
    return call(
        kernel,
        shape_of((count, query_width), bf16),
        (query, new_keys, new_values, keys_own, keys_other, values_own, values_other, limits),
        scalars=(core.reshape(1), lengths),
        grid=(grid,),
        in_specs=[rows_spec(query_width), rows_spec(head_size), rows_spec(head_size)]
        + [cache_spec] * 4
        + [limit_spec],
        out_specs=rows_spec(query_width),
        room=10,
        flops=4 * count * query_width * 2 * 2 * block_size,
    )


def out_blocks(places, attended, own, other, cut=None):
    count, width = attended.shape
    steps = places.shape[0]
    depth = own.shape[0]
    chip_width = own.shape[1] // 8

    def kernel(places_ref, attended_ref, own_ref, other_ref, *refs):
        out_refs, (held_ref, arrived) = refs[:-2], refs[-2:]
        copies = []
        for step in range(steps):
            spot = pl.ds(pl.multiple_of(places_ref[step] * chip_width, chip_width), chip_width)
            for side, weight_ref in enumerate((own_ref, other_ref)):
                target = held_ref.at[step, side * depth : (side + 1) * depth, :]
                copy = pltpu.make_async_copy(weight_ref.at[:, spot], target, arrived.at[step, side])
                copy.start()
                copies.append(copy)
        for step in range(steps):
            copies[2 * step].wait()
            copies[2 * step + 1].wait()
            product = nn(attended_ref[...], held_ref[step]).astype(bf16)
            if cut is None:
                out_refs[0][step] = product
            else:
                for ref, start, stop in zip(out_refs, (0, *cut), (*cut, count)):
                    ref[...] = product[start:stop]

    if cut is None:
        out_shape = shape_of((steps, count, chip_width), bf16)
    else:
        sizes = (cut[0], cut[1] - cut[0], count - cut[1])
        out_shape = tuple(shape_of((size, chip_width), bf16) for size in sizes)
    in_hbm = pl.BlockSpec(memory_space=pltpu.HBM)
    return call(
        kernel,
        out_shape,
        (attended, own, other),
        scalars=(places,),
        in_specs=[None, in_hbm, in_hbm],
        scratch=[
            pltpu.VMEM((steps, 2 * depth, chip_width), bf16),
            pltpu.SemaphoreType.DMA((steps, 2)),
        ],
        flops=2 * steps * count * width * chip_width,
        room=16,
    )


def plus(value, piece):
    return (value.astype(f32) + piece.astype(f32)).astype(bf16)


def second_round(blocks, from_left, from_right, from_across, cut):
    _, count, features = blocks.shape
    half = count // 2
    first, second = cut

    def kernel(blocks_ref, left_ref, right_ref, across_ref, up_ref, down_ref, over_ref):
        far, across_left, across_right = blocks_ref.at[0], blocks_ref.at[1], blocks_ref.at[2]
        up_ref[:first] = plus(across_left[:first], left_ref[...])
        up_ref[first:half] = across_left[first:half]
        up_ref[half:] = far[:half]
        down_ref[: second - half] = plus(across_right[half:second], right_ref[half - first :])
        down_ref[second - half : half] = across_right[second:]
        down_ref[half : second] = far[half:second]
        down_ref[second:] = plus(far[second:], across_ref[...])
        over_ref[:half] = across_left[half:]
        over_ref[half : half + first] = across_right[:first]
        over_ref[half + first :] = plus(across_right[first:half], right_ref[: half - first])

    sent = shape_of((count, features), bf16)
    return call(kernel, (sent, sent, sent), (blocks, from_left, from_right, from_across))


def third_round(blocks, from_left, from_right, from_across):
    _, count, features = blocks.shape
    half = count // 2

    def kernel(blocks_ref, left_ref, right_ref, across_ref, up_ref, down_ref, over_ref):
        left, right, across = blocks_ref.at[0], blocks_ref.at[1], blocks_ref.at[2]
        over_ref[:half] = plus(across[:half], left_ref[:half])
        over_ref[half:] = plus(across[half:], right_ref[:half])
        up_ref[:half] = plus(left[:half], left_ref[half:])
        up_ref[half:] = plus(left[half:], across_ref[:half])
        down_ref[:half] = plus(right[:half], across_ref[half:])
        down_ref[half:] = plus(right[half:], right_ref[half:])

    sent = shape_of((count, features), bf16)
    return call(kernel, (sent, sent, sent), (blocks, from_left, from_right, from_across))


def add_residual(core, blocks, plain, arrived):
    count, features = plain.shape
    half = features // 2

    def kernel(core_ref, blocks_ref, plain_ref, up_ref, down_ref, over_ref, keep_ref, pass_ref):
        total = blocks_ref[0].astype(f32) + up_ref[...].astype(f32)
        total += down_ref[...].astype(f32) + over_ref[...].astype(f32)
        total = plain_ref[...].astype(f32) + total
        low = core_ref[0] == 0
        first, second = total[:, :half], total[:, half:]
        keep_ref[...] = jnp.where(low, first, second).astype(bf16)
        pass_ref[...] = jnp.where(low, second, first).astype(bf16)

    part = shape_of((count, half), bf16)
    own = pl.BlockSpec((1, count, features), lambda step, core_ref: (3, 0, 0))
    return call(
        kernel,
        (part, part),
        (blocks, plain, *arrived),
        scalars=(core.reshape(1),),
        in_specs=[own] + [None] * 4,
    )


def to_steps(core, kept, got, step_count):
    count, features = kept.shape
    half_rows = count // step_count
    row_count = 2 * half_rows

    def kernel(core_ref, kept_ref, got_ref, out_ref):
        low = core_ref[0] == 0
        kept, got = kept_ref[...].astype(f32), got_ref[...].astype(f32)
        both = jnp.concatenate([jnp.where(low, kept, got), jnp.where(low, got, kept)], axis=0)
        token = lax.broadcasted_iota(i32, (2 * count, 2 * count), 0)
        column = lax.broadcasted_iota(i32, (2 * count, 2 * count), 1)
        target = token % step_count * row_count + token // step_count
        order = (column == target).astype(f32).astype(bf16)
        turned = nn(both.T.astype(bf16), order)
        for step in range(step_count):
            out_ref[step] = turned[:, step * row_count : (step + 1) * row_count].astype(bf16)

    return call(
        kernel,
        shape_of((step_count, features, row_count), bf16),
        (kept, got),
        scalars=(core.reshape(1),),
    )


def on_device(
    step_token_index,
    row_tenant_index,
    stored_lengths,
    embedding,
    input_norm_gain,
    query_weight,
    key_weight,
    value_weight,
    output_weight,
    query_norm_gain,
    key_norm_gain,
    adapter_down_weight,
    adapter_up_weight,
    stored_keys,
    stored_values,
):
    replica_count = lax.axis_size("rep")
    step_count = step_token_index.shape[0]
    row_count = row_tenant_index.shape[0]
    half_rows = row_count // 2
    count = step_count * half_rows
    own_width = embedding.shape[1]
    chip_width = 2 * own_width
    head_size = query_norm_gain.shape[0]
    me = lax.axis_index("rep")
    tp = lax.axis_index("tp")
    core = tp % 2
    chip = tp // 2

    packed = jnp.concatenate([adapter_up_weight, adapter_down_weight.transpose(0, 2, 1)], axis=2)
    slices_own = over_replicas(packed)
    key_own, value_own = key_weight.T, value_weight.T
    query_other = to_partner(query_weight)
    output_other = to_partner(output_weight)
    pair_other = to_partner(jnp.concatenate([key_own, value_own]))
    keys_other, values_other = to_partner(stored_keys), to_partner(stored_values)
    gain = input_norm_gain.reshape(8, 1, chip_width)

    def beside(sent):
        tables = row_tables(core, stored_lengths, row_tenant_index, step_count, head_size, sent)
        pairs = stack_pairs(key_own, value_own, pair_other, sent)
        slices = after(slices_own, sent)
        slices_other = to_partner(slices)
        return tables, slices, slices_other, pairs, query_other, keys_other, values_other, output_other

    tokens = step_token_index.reshape(step_count, replica_count, 2, half_rows)
    tokens = tokens.transpose(1, 2, 3, 0).reshape(replica_count, 2 * count)
    kept, passed, beside = embed(tokens, embedding.T, me, core, slices_own, beside)
    tables, *slices, pairs = beside[:4]
    own, power = to_rows(core, kept, to_partner(passed))

    z, y = chip // 4, chip % 4

    def places(*far):
        return jnp.stack([(z + dz) % 2 * 4 + (y + dy) % 4 for dz, dy in far])

    half = count // 2
    third = count // 3 // 16 * 16
    cut = (third, 2 * third)
    left, right, across = to_tp(own, 0, 1), to_tp(own, 0, -1), to_tp(own, 1, 0)
    power = power + to_tp(power, 1, 0)
    up, down, over, near = next_gather(own, left, right, across, power)
    power = after(power, over)
    up, down, over = to_tp(up, 0, 1), to_tp(down, 0, -1), to_tp(over, 1, 0)
    for mask in (1, 3):
        power = power + to_other_side(power, mask)
    last_up, last_down, last_over = last_gather(up, down, cut)
    scale, reduced = reduce_own(core, chip, own, power, gain, slices, tables, last_over)
    last_up, last_down = to_tp(last_up, 0, 1), to_tp(last_down, 0, -1)
    last_over = to_tp(last_over, 1, 0)
    reduced = reduced + to_tp(reduced, 1, 0)
    got = to_other_side(reduced, 1)
    weights = (query_weight, query_other, pairs)
    total = project(
        places((0, 0), (0, -1), (0, 1), (1, 0)),
        [[(near, index * chip_width, None)] for index in range(4)],
        scale,
        gain,
        weights,
    )
    reduced = add(reduced, got, total[2])
    got = to_other_side(reduced, 3)
    query_a, query_b, kv = project(
        places((0, 2), (1, -1), (1, 1), (1, 2)),
        [
            [(up, 0, half), (down, 0, half)],
            [(up, half, half), (over, 0, half)],
            [(over, half, half), (down, half, half)],
            [(last_up, 0, third), (last_over, 0, third), (last_down, 0, count - 2 * third)],
        ],
        scale,
        gain,
        weights,
        total,
        (reduced,),
    )
    query, new_keys, new_values = finish(
        core,
        query_a,
        query_b,
        kv,
        reduced,
        got,
        slices,
        query_norm_gain[None],
        key_norm_gain[None],
        tables,
    )

    attended = attend(
        core,
        stored_lengths,
        query,
        new_keys,
        new_values,
        (stored_keys, keys_other, stored_values, values_other),
        step_count,
    )

    out_weights = attended, output_weight, output_other
    sent = out_blocks(places((1, 2)), *out_weights, cut)
    arrived = to_tp(sent[0], 0, 1), to_tp(sent[1], 0, -1), to_tp(sent[2], 1, 0)
    blocks = out_blocks(places((0, 2), (1, 1), (1, -1)), *out_weights)
    sent = second_round(blocks, *arrived, cut)
    arrived = to_tp(sent[0], 0, 1), to_tp(sent[1], 0, -1), to_tp(sent[2], 1, 0)
    blocks = out_blocks(places((0, 1), (0, -1), (1, 0), (0, 0)), *out_weights)
    sent = third_round(blocks, *arrived)
    arrived = to_tp(sent[0], 0, 1), to_tp(sent[1], 0, -1), to_tp(sent[2], 1, 0)
    kept, passed = add_residual(core, blocks, own, arrived)
    result = to_steps(core, kept, to_partner(passed), step_count)
    return result.transpose(0, 2, 1)


def solution(mesh):
    return jax.shard_map(
        on_device,
        mesh=mesh,
        in_specs=(
            P(),
            P("rep"),
            P("rep"),
            P("rep", "tp"),
            P(),
            P(None, "tp"),
            P(None, "tp"),
            P(None, "tp"),
            P("tp", None),
            P(),
            P(),
            P(None, "tp", "rep"),
            P(None, "rep", "tp"),
            P("rep", "tp", None),
            P("rep", "tp", None),
        ),
        out_specs=P(None, "rep", "tp"),
        check_vma=False,
    )
```

```python
import jax
import jax.numpy as jnp
import numpy as np
from jax import lax
from jax.experimental import pallas as pl
from jax.experimental.pallas import tpu as pltpu
from jax.sharding import PartitionSpec as P

epsilon = 1e-06
rope_base = 1000000.0
adapter_scale = 2.0
masked_score = -1e30
slots = 128


def tp_route(dz, dy, dc):
    route = []
    for place in range(16):
        z, y, core = place // 8, place // 2 % 4, place % 2
        route.append((place, (z + dz) % 2 * 8 + (y + dy) % 4 * 2 + (core + dc) % 2))
    return route


def rep_route(dz, dx):
    return [(place, (place // 4 + dz) % 2 * 4 + (place + dx) % 4) for place in range(8)]


def to_tp(block, dz, dy):
    return lax.ppermute(block, "tp", tp_route(dz, dy, 0))


def to_partner(block):
    return lax.ppermute(block, "tp", tp_route(0, 0, 1))


def over_replicas(block):
    count = lax.axis_size("rep")
    copies = jnp.broadcast_to(block[None], (count, *block.shape))
    return lax.all_to_all(copies, "rep", 0, 0, tiled=True)


f32 = jnp.float32
bf16 = jnp.bfloat16
i32 = jnp.int32
megabyte = 1 << 20


def shape_of(shape, dtype):
    return jax.ShapeDtypeStruct(shape, dtype)


def nn(left, right):
    return jnp.dot(left, right, preferred_element_type=f32)


def nt(left, right):
    return lax.dot_general(left, right, (((1,), (1,)), ((), ())), preferred_element_type=f32)


def whole(array):
    return pl.BlockSpec(array.shape, lambda *_: (0,) * len(array.shape))


def call(kernel, out_shape, operands, scalars=(), grid=(1,), in_specs=None, out_specs=None, **extra):
    if in_specs is None:
        in_specs = [None] * len(operands)
    in_specs = [spec or whole(operand) for spec, operand in zip(in_specs, operands)]
    if out_specs is None:
        out_specs = jax.tree.map(whole, out_shape)
    flops = extra.pop("flops", 1 << 20)
    scratch = extra.pop("scratch", [])
    room = extra.pop("room", 8)
    moved = sum(operand.size * operand.dtype.itemsize for operand in operands)
    return pl.pallas_call(
        kernel,
        out_shape=out_shape,
        grid_spec=pltpu.PrefetchScalarGridSpec(
            num_scalar_prefetch=len(scalars),
            grid=grid,
            in_specs=in_specs,
            out_specs=out_specs,
            scratch_shapes=scratch,
        ),
        compiler_params=pltpu.CompilerParams(vmem_limit_bytes=room * megabyte),
        cost_estimate=pl.CostEstimate(flops=flops, bytes_accessed=moved, transcendentals=0),
    )(*scalars, *operands)


def after(value, *others):
    def kernel(*refs):
        del refs

    anywhere = pl.BlockSpec(memory_space=pl.ANY)
    return pl.pallas_call(
        kernel,
        out_shape=shape_of(value.shape, value.dtype),
        in_specs=[anywhere] * (1 + len(others)),
        out_specs=anywhere,
        input_output_aliases={0: 0},
    )(value, *others)


def row_tables(core, lengths, tenants, step_count, head_size, *others):
    row_count = lengths.shape[0]
    count = row_count // 2 * step_count
    half_dim = head_size // 2
    inverse = rope_base ** (-np.arange(half_dim, dtype=np.float32) / np.float32(half_dim))
    inverse = np.concatenate([inverse, inverse]).astype(np.float32)[None]

    def kernel(core_ref, lengths_ref, tenants_ref, inverse_ref, *refs):
        out_ref = refs[-1]
        token = lax.broadcasted_iota(i32, (count, row_count), 0)
        row = lax.broadcasted_iota(i32, (count, row_count), 1)
        chosen = row == core_ref[0] * (row_count // 2) + token // step_count
        length = jnp.sum(jnp.where(chosen, lengths_ref[...], 0).astype(f32), axis=1, keepdims=True)
        tenant = jnp.sum(jnp.where(chosen, tenants_ref[...], 0).astype(f32), axis=1, keepdims=True)
        step = lax.broadcasted_iota(i32, (count, 1), 0) % step_count
        angle = (length + step.astype(f32)) * inverse_ref[...]
        lane = lax.broadcasted_iota(i32, (count, head_size), 1)
        out_ref[:, :head_size] = jnp.cos(angle)
        sine = jnp.sin(angle)
        out_ref[:, head_size : 2 * head_size] = jnp.where(lane < half_dim, -sine, sine)
        out_ref[:, 2 * head_size :] = jnp.broadcast_to(tenant, (count, head_size))

    return call(
        kernel,
        shape_of((count, 3 * head_size), f32),
        (lengths[None], tenants[None], inverse, *others),
        scalars=(core.reshape(1),),
        in_specs=[None] * 3 + [pl.BlockSpec(memory_space=pl.ANY)] * len(others),
    )


def ranks(tokens, me, vocab_rows):
    parts, count = tokens.shape

    def kernel(me_ref, tokens_ref, rank_ref, most_ref):
        owner = tokens_ref[...] // vocab_rows
        own = tokens_ref[pl.ds(me_ref[0], 1), :] // vocab_rows
        from_part = lax.broadcasted_iota(i32, (parts, count), 0) == own
        wanted = jnp.concatenate([(owner == me_ref[0]).astype(f32), from_part.astype(f32)], axis=0)
        earlier = lax.broadcasted_iota(i32, (count, count), 0) < lax.broadcasted_iota(
            i32, (count, count), 1
        )
        rank = nn(wanted.astype(bf16), earlier.astype(f32).astype(bf16)).astype(i32)
        rank_ref[...] = jnp.where(wanted > 0, rank, -1)
        most = jnp.zeros((parts, 1), f32)
        for part in range(parts):
            found = jnp.sum((owner == part).astype(f32), axis=1, keepdims=True)
            most = jnp.maximum(most, found)
        most_ref[0] = jnp.max(most).astype(i32)

    return call(
        kernel,
        (shape_of((2 * parts, count), i32), shape_of((1,), i32)),
        (tokens,),
        scalars=(me.reshape(1),),
        out_specs=(
            whole(shape_of((2 * parts, count), i32)),
            pl.BlockSpec(memory_space=pltpu.SMEM),
        ),
    )


def pick(tokens, rank, table, me, base):
    parts, count = tokens.shape
    features, vocab_rows = table.shape
    tile, piece = 2432, 128
    steps = pl.cdiv(vocab_rows, tile)

    def kernel(me_ref, base_ref, tokens_ref, rank_ref, table_ref, out_ref, list_ref, total_ref):
        step = pl.program_id(0)

        @pl.when(step == 0)
        def _():
            place = base_ref[0] + lax.broadcasted_iota(i32, (slots, count), 0)
            for part in range(parts):
                local = tokens_ref[part : part + 1, :] - me_ref[0] * vocab_rows
                hit = (rank_ref[part : part + 1, :] == place).astype(f32).astype(bf16)
                inside = jnp.logical_and(local >= 0, local < vocab_rows)
                local = jnp.where(inside, local, 0)
                high = local // 128
                digits = jnp.concatenate(
                    [high, local - high * 128, jnp.ones((6, count), i32)], axis=0
                )
                found = nt(digits.astype(f32).astype(bf16), hit).astype(i32)
                name = found[0:1] * 128 + found[1:2]
                list_ref[part : part + 1, :] = jnp.where(found[2:3] > 0, name, -1)
            total_ref[...] = jnp.zeros_like(total_ref)

        def add(block):
            name = lax.broadcasted_iota(i32, (piece, slots), 0).astype(f32).astype(bf16)
            yes, no = jnp.ones((), bf16), jnp.zeros((), bf16)
            for part in range(0, parts, 2):
                chosen = []
                for side in (part, part + 1):
                    rows = []
                    for start in range(0, tile, piece):
                        wanted = list_ref[side : side + 1, :] - (step * tile + start)
                        wanted = jnp.clip(wanted, -1, piece).astype(f32).astype(bf16)
                        rows.append(jnp.where(name == wanted, yes, no))
                    chosen.append(jnp.concatenate(rows, axis=0))
                total_ref[:, part * slots : (part + 2) * slots] += nn(
                    block, jnp.concatenate(chosen, axis=1)
                )

        @pl.when(step < steps - 1)
        def _():
            add(table_ref[...])

        @pl.when(step == steps - 1)
        def _():
            lane = step * tile + lax.broadcasted_iota(i32, (1, tile), 1)
            add(jnp.where(lane < vocab_rows, table_ref[...].astype(f32), 0.0).astype(bf16))

        @pl.when(step == steps - 1)
        def _():
            for part in range(parts):
                out_ref[part] = total_ref[:, part * slots : (part + 1) * slots].astype(bf16)

    return call(
        kernel,
        shape_of((parts, features, slots), bf16),
        (tokens, rank, table),
        scalars=(me.reshape(1), base.reshape(1)),
        grid=(steps,),
        in_specs=[None, None, pl.BlockSpec((features, tile), lambda step, *_: (0, step))],
        scratch=[pltpu.VMEM((parts, slots), i32), pltpu.VMEM((features, parts * slots), f32)],
        flops=2 * features * vocab_rows * parts * slots,
        room=12,
    )


def place_slots(core, rank, got, base, others=()):
    parts, features, _ = got.shape
    count = rank.shape[1]
    half = count // 2

    def kernel(core_ref, base_ref, rank_ref, got_ref, *refs):
        kept_ref, passed_ref = refs[-2:]
        place = base_ref[0] + lax.broadcasted_iota(i32, (slots, count), 0)
        total = jnp.zeros((features, count), f32)
        for part in range(parts):
            hit = rank_ref[parts + part : parts + part + 1, :] == place
            total += nn(got_ref[part], hit.astype(f32).astype(bf16))
        low = core_ref[0] == 0
        first, second = total[:, :half], total[:, half:]
        kept_ref[...] = jnp.where(low, first, second).astype(bf16)
        passed_ref[...] = jnp.where(low, second, first).astype(bf16)

    columns = shape_of((features, half), bf16)
    return call(
        kernel,
        (columns, columns),
        (rank, got, *others),
        scalars=(core.reshape(1), base.reshape(1)),
        in_specs=[None, None] + [pl.BlockSpec(memory_space=pl.ANY)] * len(others),
    )


def embed(tokens, table, me, core, beside):
    rank, most = ranks(tokens, me, table.shape[1])

    def more(state):
        base, kept, passed = state
        sent = pick(tokens, rank, table, me, base)
        got = lax.all_to_all(sent, "rep", 0, 0, tiled=True)
        more_kept, more_passed = place_slots(core, rank, got, base)
        return base + slots, kept + more_kept, passed + more_passed

    base = jnp.zeros((), i32)
    sent = pick(tokens, rank, table, me, base)
    got = lax.all_to_all(sent, "rep", 0, 0, tiled=True)
    beside = beside(sent)
    first = place_slots(core, rank, got, base, beside)
    _, kept, passed = lax.while_loop(
        lambda state: state[0] < most[0], more, (jnp.full((), slots, i32), *first)
    )
    return kept, passed, beside


def to_rows(core, kept, got):
    features, count = kept.shape

    def kernel(core_ref, kept_ref, got_ref, plain_ref, power_ref):
        low = core_ref[0] == 0
        kept, got = kept_ref[...].astype(f32), got_ref[...].astype(f32)
        both = jnp.concatenate([jnp.where(low, kept, got), jnp.where(low, got, kept)], axis=0)
        plain_ref[...] = both.T.astype(bf16)
        power = jnp.sum(both * both, axis=0, keepdims=True)
        for part in range(count // 128):
            power_ref[part : part + 1, :] = power[:, part * 128 : (part + 1) * 128]

    return call(
        kernel,
        (shape_of((count, 2 * features), bf16), shape_of((count // 128, 128), f32)),
        (kept, got),
        scalars=(core.reshape(1),),
    )


def stack_pairs(key, value, other, ready):
    rows, columns = key.shape
    tile = columns // 4

    def kernel(key_ref, value_ref, other_ref, ready_ref, out_ref):
        del ready_ref
        out_ref[:rows] = key_ref[...]
        out_ref[rows : 2 * rows] = other_ref[:rows]
        out_ref[2 * rows : 3 * rows] = value_ref[...]
        out_ref[3 * rows :] = other_ref[rows:]

    tall = lambda many: pl.BlockSpec((many * rows, tile), lambda step: (0, step))
    return call(
        kernel,
        shape_of((4 * rows, columns), bf16),
        (key, value, other, ready),
        grid=(4,),
        in_specs=[tall(1), tall(1), tall(2), pl.BlockSpec(memory_space=pl.ANY)],
        out_specs=tall(4),
    )


def to_other_side(value, mask):
    route = [(place, place ^ (mask << 1)) for place in range(16)]
    return lax.ppermute(value, "tp", route)


def reduce_own(core, chip, plain, power, gain, slices, tables, *others):
    count, features = plain.shape
    width = gain.size
    parts, tenant_count, rank_part, packed_width = slices[0].shape
    skip = packed_width - features // 2

    def kernel(
        core_ref, chip_ref, plain_ref, power_ref, gain_ref, own_ref, other_ref, tables_ref, *refs,
    ):
        scale_ref, out_ref = refs[-2:]
        tenant_rows = tables_ref[:, 2 * 128 :]
        low = core_ref[0] == 0
        scale = lax.rsqrt(power_ref[...] / width + epsilon)
        scale = jnp.concatenate(
            [
                jnp.broadcast_to(scale[part : part + 1, :], (128, 128)).T
                for part in range(count // 128)
            ],
            axis=0,
        )
        scale_ref[...] = scale
        normed = (plain_ref[...].astype(f32) * scale[:, :1] * gain_ref[0]).astype(bf16)
        reduced = jnp.zeros((count, parts * rank_part), f32)
        for tenant in range(tenant_count):
            own, other = [
                jnp.concatenate([ref[part, tenant, :, skip:] for part in range(parts)], axis=0)
                for ref in (own_ref, other_ref)
            ]
            own, other = own.astype(f32), other.astype(f32)
            down = jnp.concatenate(
                [jnp.where(low, own, other), jnp.where(low, other, own)], axis=1
            ).astype(bf16)
            reduced += jnp.where(tenant_rows == tenant, nt(normed, down), 0.0)
        out_ref[...] = reduced

    return call(
        kernel,
        (shape_of((count, 128), f32), shape_of((count, parts * rank_part), f32)),
        (plain, power, gain, *slices, tables, *others),
        scalars=(core.reshape(1), chip.reshape(1)),
        in_specs=[
            None,
            None,
            pl.BlockSpec((1, 1, features), lambda step, core, chip: (chip[0], 0, 0)),
        ]
        + [None] * 3
        + [pl.BlockSpec(memory_space=pl.ANY)] * len(others),
        flops=2 * features * count * parts * tenant_count * rank_part,
        room=12,
    )


def next_gather(own, left, right, across, *others):
    count, features = left.shape
    half = count // 2

    def kernel(own_ref, left_ref, right_ref, across_ref, *refs):
        up_ref, down_ref, over_ref, near_ref = refs[-4:]
        up_ref[:half] = left_ref[:half]
        up_ref[half:] = across_ref[:half]
        down_ref[:half] = right_ref[half:]
        down_ref[half:] = across_ref[half:]
        over_ref[:half] = left_ref[half:]
        over_ref[half:] = right_ref[:half]
        for index, ref in enumerate((own_ref, left_ref, right_ref, across_ref)):
            near_ref[:, index * features : (index + 1) * features] = ref[...]

    sent = shape_of(left.shape, bf16)
    return call(
        kernel,
        (sent, sent, sent, shape_of((count, 4 * features), bf16)),
        (own, left, right, across, *others),
        in_specs=[None] * 4 + [pl.BlockSpec(memory_space=pl.ANY)] * len(others),
    )


def last_gather(up, down, cut):
    count, features = up.shape
    half = count // 2
    first, second = cut

    def kernel(up_ref, down_ref, right_ref, left_ref, across_ref):
        right_ref[...] = up_ref[half : half + first]
        left_ref[...] = down_ref[second:]
        across_ref[: half - first] = up_ref[first:half]
        across_ref[half - first :] = down_ref[: second - half]

    return call(
        kernel,
        tuple(
            shape_of((rows, features), bf16) for rows in (first, count - second, second - first)
        ),
        (up, down),
    )


def project(places, pieces, scale, gain, weights, total=None, others=()):
    arrays = []
    layout = []
    for piece in pieces:
        entry = []
        for array, start, rows in piece:
            known = [index for index, held in enumerate(arrays) if held is array]
            if not known:
                arrays.append(array)
                known = [len(arrays) - 1]
            entry.append((known[0], start, rows))
        layout.append(entry)
    count = scale.shape[0]
    query_own, query_other, pairs = weights
    columns = query_own.shape[1]
    chip_width = query_own.shape[0] // 8
    has_total = total is not None
    steps = 2
    part = columns // steps
    many = len(pieces)

    def kernel(places_ref, *refs):
        del places_ref
        refs = list(refs)
        taken = [refs.pop(0) for _ in arrays]
        scale_ref = refs.pop(0)
        gain_refs = [refs.pop(0) for _ in pieces]
        own_refs = [refs.pop(0) for _ in pieces]
        other_refs = [refs.pop(0) for _ in pieces]
        pair_refs = [refs.pop(0) for _ in pieces]
        total_refs = [refs.pop(0) for _ in range(3)] if has_total else None
        sums = refs[-3:]
        step = pl.program_id(0)
        rows = []
        for entry, gain_ref in zip(layout, gain_refs):
            plain = [
                taken[at][:, first : first + chip_width]
                if size is None
                else taken[at][first : first + size]
                for at, first, size in entry
            ]
            plain = jnp.concatenate(plain, axis=0).astype(f32)
            rows.append((plain * scale_ref[:, :1] * gain_ref[0]).astype(bf16))
        rows = jnp.concatenate(rows, axis=1)
        for side, weight_refs in enumerate((own_refs, other_refs)):
            result = nn(rows, jnp.concatenate([ref[...] for ref in weight_refs], axis=0))
            if has_total:
                result += total_refs[side][...]
            sums[side][...] = result

        @pl.when(step == 0)
        def _():
            result = nt(rows, jnp.concatenate([ref[...] for ref in pair_refs], axis=1))
            if has_total:
                result += total_refs[2][...]
            sums[2][...] = result

    def weight_spec(index):
        return pl.BlockSpec((chip_width, part), lambda step, places: (places[index], step))

    def pair_spec(index):
        return pl.BlockSpec((pairs.shape[0], chip_width), lambda step, places: (0, places[index]))

    sum_spec = pl.BlockSpec((count, part), lambda step, places: (0, step))
    sums = (
        shape_of((count, columns), f32),
        shape_of((count, columns), f32),
        shape_of((count, pairs.shape[0]), f32),
    )
    sum_specs = (sum_spec, sum_spec, whole(sums[2]))
    def gain_spec(index):
        return pl.BlockSpec((1, 1, chip_width), lambda step, places: (places[index], 0, 0))

    in_specs = [None] * (len(arrays) + 1)
    in_specs += [gain_spec(index) for index in range(many)]
    in_specs += [weight_spec(index) for index in range(many)] * 2
    in_specs += [pair_spec(index) for index in range(many)]
    operands = arrays + [scale] + [gain] * many + [query_own] * many + [query_other] * many + [pairs] * many
    if has_total:
        operands += list(total)
        in_specs += list(sum_specs)
    operands += list(others)
    in_specs += [pl.BlockSpec(memory_space=pl.ANY)] * len(others)
    return call(
        kernel,
        sums,
        operands,
        scalars=(places,),
        grid=(steps,),
        in_specs=in_specs,
        out_specs=sum_specs,
        flops=2 * many * count * chip_width * (2 * columns + pairs.shape[0]),
        room=18,
    )


def add(value, piece, *others):
    def kernel(value_ref, piece_ref, *refs):
        refs[-1][...] = value_ref[...] + piece_ref[...]

    return call(
        kernel,
        shape_of(value.shape, value.dtype),
        (value, piece, *others),
        in_specs=[None, None] + [pl.BlockSpec(memory_space=pl.ANY)] * len(others),
    )


def finish(core, query_own, query_other, kv, reduced, got, slices, query_gain, key_gain, tables):
    count, columns = query_own.shape

    def kernel(core_ref, own_ref, other_ref, kv_ref, *refs):
        finish_kernel(core_ref, (own_ref, other_ref), kv_ref, refs[:7], refs[7:])

    rows = shape_of((count, kv.shape[1] // 2), bf16)
    return call(
        kernel,
        (shape_of((count, 2 * columns), f32), rows, rows),
        (query_own, query_other, kv, reduced, got, *slices, query_gain, key_gain, tables),
        scalars=(core.reshape(1),),
        flops=2 << 30,
        room=16,
    )


def finish_kernel(core_ref, query_refs, kv_ref, refs, outs):
    reduced_ref, got_ref, *slice_refs = refs[:4]
    query_gain_ref, key_gain_ref, tables_ref = refs[4:]
    head_size = query_gain_ref.shape[1]
    cosine, sine = tables_ref[:, :head_size], tables_ref[:, head_size : 2 * head_size]
    tenant_rows = tables_ref[:, 2 * head_size :]
    out_query_ref, out_key_ref, out_value_ref = outs
    parts, tenant_count = slice_refs[0].shape[:2]
    columns = query_refs[0].shape[1]
    low_rank = (reduced_ref[...] + got_ref[...]).astype(bf16).astype(f32)
    def head_norm(vector, gain):
        power = jnp.mean(vector * vector, axis=-1, keepdims=True)
        vector = vector * lax.rsqrt(power + epsilon) * gain
        return vector * cosine + pltpu.roll(vector, head_size // 2, 1) * sine

    spread = jnp.concatenate(
        [
            jnp.where(tenant_rows == tenant, low_rank, 0.0).astype(bf16)
            for tenant in range(tenant_count)
        ],
        axis=1,
    )
    for side, up_ref in enumerate(slice_refs):
        up = jnp.concatenate(
            [
                up_ref[part, tenant, :, :columns]
                for tenant in range(tenant_count)
                for part in range(parts)
            ],
            axis=0,
        )
        delta = nn(spread, up)
        for head in range(columns // head_size):
            near = slice(head * head_size, (head + 1) * head_size)
            spot = slice(side * columns + near.start, side * columns + near.stop)
            query = query_refs[side][:, near] + adapter_scale * delta[:, near]
            query = head_norm(query, query_gain_ref[...])
            out_query_ref[:, spot] = query.astype(bf16).astype(f32)
    low = core_ref[0] == 0
    both = kv_ref[...]
    key = both[:, :head_size].astype(bf16).astype(f32)
    value = both[:, head_size:]
    key = jnp.where(low, key, pltpu.roll(key, head_size // 2, 1))
    value = jnp.where(low, value, pltpu.roll(value, head_size // 2, 1))
    out_key_ref[...] = head_norm(key, key_gain_ref[...]).astype(bf16)
    out_value_ref[...] = value.astype(bf16)


def allowed_below(block_size, step_count, group):
    table = np.full((2, 2, group * 2 * step_count, 4 * block_size + 4 * step_count), 1 << 20, np.int32)
    for row in range(table.shape[2]):
        pair_row, step = row // step_count % 2, row % step_count
        for core in range(2):
            for side in range(2):
                start = side * 2 * block_size + pair_row * block_size
                first = (core if side == 0 else 1 - core) * block_size
                table[core, :, row, start : start + block_size] = first + np.arange(block_size)
            for pair in range(2):
                start = 4 * block_size + (2 * pair + pair_row) * step_count
                table[core, pair, row, start : start + step + 1] = -1
    return table


def attend(core, lengths, query, new_keys, new_values, caches, step_count):
    count, query_width = query.shape
    block_size, head_size = caches[0].shape[1:]
    group = query_width // head_size
    rows_a_step = 32
    block = rows_a_step * step_count
    half_rows = count // step_count
    grid = half_rows // rows_a_step
    score_scale = head_size ** (-0.5)
    limits = allowed_below(block_size, step_count, group)

    def kernel(
        core_ref, lengths_ref, query_ref, new_key_ref, new_value_ref, own_key_ref, other_key_ref,
        own_value_ref, other_value_ref, limit_ref, out_ref,
    ):
        first = core_ref[0] * half_rows + pl.program_id(0) * rows_a_step
        pair_tokens = 2 * step_count
        pairs = range(rows_a_step // 2)
        row = lax.broadcasted_iota(i32, (group * pair_tokens, 1), 0) // step_count % 2
        fresh = [slice(pair // 2 * 4 * step_count, (pair // 2 + 1) * 4 * step_count) for pair in pairs]

        def joined(pair, own, other, new):
            near = 2 * pair
            return jnp.concatenate(
                [own[near], own[near + 1], other[near], other[near + 1], new[fresh[pair], :]], axis=0
            )

        scores = []
        for pair in pairs:
            tokens = slice(pair * pair_tokens, (pair + 1) * pair_tokens)
            queries = [
                query_ref[tokens, head * head_size : (head + 1) * head_size] for head in range(group)
            ]
            queries = jnp.concatenate(queries, axis=0).astype(bf16)
            scores.append(nt(queries, joined(pair, own_key_ref, other_key_ref, new_key_ref)))
        weights, totals = [], []
        for pair in pairs:
            length = jnp.where(
                row == 0, lengths_ref[first + 2 * pair], lengths_ref[first + 2 * pair + 1]
            )
            seen = limit_ref[0, pair % 2] < length
            masked = jnp.where(seen, scores[pair] * score_scale, masked_score)
            weight = jnp.exp(masked - jnp.max(masked, axis=1, keepdims=True))
            totals.append(jnp.sum(weight, axis=1, keepdims=True))
            weights.append(weight.astype(bf16))
        results = []
        for pair in pairs:
            values = joined(pair, own_value_ref, other_value_ref, new_value_ref)
            results.append(nn(weights[pair], values) / totals[pair])
        for pair in pairs[::2]:
            for head in range(group):
                part = slice(head * pair_tokens, (head + 1) * pair_tokens)
                both = jnp.concatenate([results[pair][part], results[pair + 1][part]], axis=0)
                out_ref[fresh[pair], head * head_size : (head + 1) * head_size] = both.astype(bf16)

    rows_spec = lambda width: pl.BlockSpec((block, width), lambda step, *_: (step, 0))
    cache_spec = pl.BlockSpec(
        (rows_a_step, block_size, head_size),
        lambda step, core_ref, lengths_ref: (core_ref[0] * grid + step, 0, 0),
    )
    limit_spec = pl.BlockSpec(
        (1, *limits.shape[1:]), lambda step, core_ref, lengths_ref: (core_ref[0], 0, 0, 0)
    )
    keys_own, keys_other, values_own, values_other = caches
    return call(
        kernel,
        shape_of((count, query_width), bf16),
        (query, new_keys, new_values, keys_own, keys_other, values_own, values_other, limits),
        scalars=(core.reshape(1), lengths),
        grid=(grid,),
        in_specs=[rows_spec(query_width), rows_spec(head_size), rows_spec(head_size)]
        + [cache_spec] * 4
        + [limit_spec],
        out_specs=rows_spec(query_width),
        room=32,
        flops=4 * count * query_width * 2 * 2 * block_size,
    )


def out_blocks(places, attended, own, other, cut=None):
    count, width = attended.shape
    steps = places.shape[0]
    depth = own.shape[0]
    chip_width = own.shape[1] // 8

    def kernel(places_ref, attended_ref, own_ref, other_ref, *refs):
        out_refs, (held_ref, arrived) = refs[:-2], refs[-2:]
        copies = []
        for step in range(steps):
            spot = pl.ds(pl.multiple_of(places_ref[step] * chip_width, chip_width), chip_width)
            for side, weight_ref in enumerate((own_ref, other_ref)):
                target = held_ref.at[step, side * depth : (side + 1) * depth, :]
                copy = pltpu.make_async_copy(weight_ref.at[:, spot], target, arrived.at[step, side])
                copy.start()
                copies.append(copy)
        for step in range(steps):
            copies[2 * step].wait()
            copies[2 * step + 1].wait()
            product = nn(attended_ref[...], held_ref[step]).astype(bf16)
            if cut is None:
                out_refs[0][step] = product
            else:
                for ref, start, stop in zip(out_refs, (0, *cut), (*cut, count)):
                    ref[...] = product[start:stop]

    if cut is None:
        out_shape = shape_of((steps, count, chip_width), bf16)
    else:
        sizes = (cut[0], cut[1] - cut[0], count - cut[1])
        out_shape = tuple(shape_of((size, chip_width), bf16) for size in sizes)
    in_hbm = pl.BlockSpec(memory_space=pltpu.HBM)
    return call(
        kernel,
        out_shape,
        (attended, own, other),
        scalars=(places,),
        in_specs=[None, in_hbm, in_hbm],
        scratch=[
            pltpu.VMEM((steps, 2 * depth, chip_width), bf16),
            pltpu.SemaphoreType.DMA((steps, 2)),
        ],
        flops=2 * steps * count * width * chip_width,
        room=16,
    )


def plus(value, piece):
    return (value.astype(f32) + piece.astype(f32)).astype(bf16)


def second_round(blocks, from_left, from_right, from_across, cut):
    _, count, features = blocks.shape
    half = count // 2
    first, second = cut

    def kernel(blocks_ref, left_ref, right_ref, across_ref, up_ref, down_ref, over_ref):
        far, across_left, across_right = blocks_ref.at[0], blocks_ref.at[1], blocks_ref.at[2]
        up_ref[:first] = plus(across_left[:first], left_ref[...])
        up_ref[first:half] = across_left[first:half]
        up_ref[half:] = far[:half]
        down_ref[: second - half] = plus(across_right[half:second], right_ref[half - first :])
        down_ref[second - half : half] = across_right[second:]
        down_ref[half : second] = far[half:second]
        down_ref[second:] = plus(far[second:], across_ref[...])
        over_ref[:half] = across_left[half:]
        over_ref[half : half + first] = across_right[:first]
        over_ref[half + first :] = plus(across_right[first:half], right_ref[: half - first])

    sent = shape_of((count, features), bf16)
    return call(kernel, (sent, sent, sent), (blocks, from_left, from_right, from_across))


def third_round(blocks, from_left, from_right, from_across):
    _, count, features = blocks.shape
    half = count // 2

    def kernel(blocks_ref, left_ref, right_ref, across_ref, up_ref, down_ref, over_ref):
        left, right, across = blocks_ref.at[0], blocks_ref.at[1], blocks_ref.at[2]
        over_ref[:half] = plus(across[:half], left_ref[:half])
        over_ref[half:] = plus(across[half:], right_ref[:half])
        up_ref[:half] = plus(left[:half], left_ref[half:])
        up_ref[half:] = plus(left[half:], across_ref[:half])
        down_ref[:half] = plus(right[:half], across_ref[half:])
        down_ref[half:] = plus(right[half:], right_ref[half:])

    sent = shape_of((count, features), bf16)
    return call(kernel, (sent, sent, sent), (blocks, from_left, from_right, from_across))


def add_residual(core, blocks, plain, arrived):
    count, features = plain.shape
    half = features // 2

    def kernel(core_ref, blocks_ref, plain_ref, up_ref, down_ref, over_ref, keep_ref, pass_ref):
        total = blocks_ref[0].astype(f32) + up_ref[...].astype(f32)
        total += down_ref[...].astype(f32) + over_ref[...].astype(f32)
        total = plain_ref[...].astype(f32) + total
        low = core_ref[0] == 0
        first, second = total[:, :half], total[:, half:]
        keep_ref[...] = jnp.where(low, first, second).astype(bf16)
        pass_ref[...] = jnp.where(low, second, first).astype(bf16)

    part = shape_of((count, half), bf16)
    own = pl.BlockSpec((1, count, features), lambda step, core_ref: (3, 0, 0))
    return call(
        kernel,
        (part, part),
        (blocks, plain, *arrived),
        scalars=(core.reshape(1),),
        in_specs=[own] + [None] * 4,
    )


def to_steps(core, kept, got, step_count):
    count, features = kept.shape
    half_rows = count // step_count
    row_count = 2 * half_rows

    def kernel(core_ref, kept_ref, got_ref, out_ref):
        low = core_ref[0] == 0
        kept, got = kept_ref[...].astype(f32), got_ref[...].astype(f32)
        both = jnp.concatenate([jnp.where(low, kept, got), jnp.where(low, got, kept)], axis=0)
        token = lax.broadcasted_iota(i32, (2 * count, 2 * count), 0)
        column = lax.broadcasted_iota(i32, (2 * count, 2 * count), 1)
        target = token % step_count * row_count + token // step_count
        order = (column == target).astype(f32).astype(bf16)
        turned = nn(both.T.astype(bf16), order)
        for step in range(step_count):
            out_ref[step] = turned[:, step * row_count : (step + 1) * row_count].astype(bf16)

    return call(
        kernel,
        shape_of((step_count, features, row_count), bf16),
        (kept, got),
        scalars=(core.reshape(1),),
    )


def on_device(
    step_token_index,
    row_tenant_index,
    stored_lengths,
    embedding,
    input_norm_gain,
    query_weight,
    key_weight,
    value_weight,
    output_weight,
    query_norm_gain,
    key_norm_gain,
    adapter_down_weight,
    adapter_up_weight,
    stored_keys,
    stored_values,
):
    replica_count = lax.axis_size("rep")
    step_count = step_token_index.shape[0]
    row_count = row_tenant_index.shape[0]
    half_rows = row_count // 2
    count = step_count * half_rows
    own_width = embedding.shape[1]
    chip_width = 2 * own_width
    head_size = query_norm_gain.shape[0]
    me = lax.axis_index("rep")
    tp = lax.axis_index("tp")
    core = tp % 2
    chip = tp // 2

    packed = jnp.concatenate([adapter_up_weight, adapter_down_weight.transpose(0, 2, 1)], axis=2)
    slices_own = over_replicas(packed)
    key_own, value_own = key_weight.T, value_weight.T
    query_other = to_partner(query_weight)
    output_other = to_partner(output_weight)
    pair_other = to_partner(jnp.concatenate([key_own, value_own]))
    keys_other, values_other = to_partner(stored_keys), to_partner(stored_values)
    gain = input_norm_gain.reshape(8, 1, chip_width)

    def beside(sent):
        tables = row_tables(core, stored_lengths, row_tenant_index, step_count, head_size, sent)
        pairs = stack_pairs(key_own, value_own, pair_other, sent)
        slices = after(slices_own, sent)
        slices_other = to_partner(slices)
        return tables, slices, slices_other, pairs, query_other, keys_other, values_other, output_other

    tokens = step_token_index.reshape(step_count, replica_count, 2, half_rows)
    tokens = tokens.transpose(1, 2, 3, 0).reshape(replica_count, 2 * count)
    kept, passed, beside = embed(tokens, embedding.T, me, core, beside)
    tables, *slices, pairs = beside[:4]
    own, power = to_rows(core, kept, to_partner(passed))

    z, y = chip // 4, chip % 4

    def places(*far):
        return jnp.stack([(z + dz) % 2 * 4 + (y + dy) % 4 for dz, dy in far])

    half = count // 2
    third = count // 3 // 16 * 16
    cut = (third, 2 * third)
    left, right, across = to_tp(own, 0, 1), to_tp(own, 0, -1), to_tp(own, 1, 0)
    power = power + to_tp(power, 1, 0)
    up, down, over, near = next_gather(own, left, right, across, power)
    power = after(power, over)
    up, down, over = to_tp(up, 0, 1), to_tp(down, 0, -1), to_tp(over, 1, 0)
    for mask in (1, 3):
        power = power + to_other_side(power, mask)
    last_up, last_down, last_over = last_gather(up, down, cut)
    scale, reduced = reduce_own(core, chip, own, power, gain, slices, tables, last_over)
    last_up, last_down = to_tp(last_up, 0, 1), to_tp(last_down, 0, -1)
    last_over = to_tp(last_over, 1, 0)
    reduced = reduced + to_tp(reduced, 1, 0)
    got = to_other_side(reduced, 1)
    weights = (query_weight, query_other, pairs)
    total = project(
        places((0, 0), (0, -1), (0, 1), (1, 0)),
        [[(near, index * chip_width, None)] for index in range(4)],
        scale,
        gain,
        weights,
    )
    reduced = add(reduced, got, total[2])
    got = to_other_side(reduced, 3)
    query_a, query_b, kv = project(
        places((0, 2), (1, -1), (1, 1), (1, 2)),
        [
            [(up, 0, half), (down, 0, half)],
            [(up, half, half), (over, 0, half)],
            [(over, half, half), (down, half, half)],
            [(last_up, 0, third), (last_over, 0, third), (last_down, 0, count - 2 * third)],
        ],
        scale,
        gain,
        weights,
        total,
        (reduced,),
    )
    query, new_keys, new_values = finish(
        core,
        query_a,
        query_b,
        kv,
        reduced,
        got,
        slices,
        query_norm_gain[None],
        key_norm_gain[None],
        tables,
    )

    attended = attend(
        core,
        stored_lengths,
        query,
        new_keys,
        new_values,
        (stored_keys, keys_other, stored_values, values_other),
        step_count,
    )

    out_weights = attended, output_weight, output_other
    sent = out_blocks(places((1, 2)), *out_weights, cut)
    arrived = to_tp(sent[0], 0, 1), to_tp(sent[1], 0, -1), to_tp(sent[2], 1, 0)
    blocks = out_blocks(places((0, 2), (1, 1), (1, -1)), *out_weights)
    sent = second_round(blocks, *arrived, cut)
    arrived = to_tp(sent[0], 0, 1), to_tp(sent[1], 0, -1), to_tp(sent[2], 1, 0)
    blocks = out_blocks(places((0, 1), (0, -1), (1, 0), (0, 0)), *out_weights)
    sent = third_round(blocks, *arrived)
    arrived = to_tp(sent[0], 0, 1), to_tp(sent[1], 0, -1), to_tp(sent[2], 1, 0)
    kept, passed = add_residual(core, blocks, own, arrived)
    result = to_steps(core, kept, to_partner(passed), step_count)
    return result.transpose(0, 2, 1)


def solution(mesh):
    return jax.shard_map(
        on_device,
        mesh=mesh,
        in_specs=(
            P(),
            P("rep"),
            P("rep"),
            P("rep", "tp"),
            P(),
            P(None, "tp"),
            P(None, "tp"),
            P(None, "tp"),
            P("tp", None),
            P(),
            P(),
            P(None, "tp", "rep"),
            P(None, "rep", "tp"),
            P("rep", "tp", None),
            P("rep", "tp", None),
        ),
        out_specs=P(None, "rep", "tp"),
        check_vma=False,
    )
```
